32 devices in a mesh: groups: 2 (over y), leaf: 4 (over x, core), inner: 4 (over z).
Axes of the slice: x: 2, y: 2, z: 4, core: 2. Of those that a mesh axis runs over, the one named last changes fastest.
Arguments:
- embed: bfloat16 [12288, 256], P(('groups', 'leaf', 'inner')), parts along dimension 0, may hold values from -1.5 to 1.5
- factors: bfloat16 [3, 12288, 128], P(None, ('groups', 'leaf', 'inner')), parts along dimension 1
- targets: float32 [12288, 32], P(('groups', 'leaf', 'inner')), parts along dimension 0
Outputs:
- solution: float32 [12288, 32], P(('groups', 'leaf', 'inner')), parts along dimension 0
- residual: float32 [12288, 32], P(('groups', 'leaf', 'inner')), parts along dimension 0
The draws below stay inside these ranges and needn't reach their ends.
There are 2 independent parts, one for each index of `groups`. The reference program is written for one: setup_inputs(seed, part) draws one part's arguments, and reference() takes and returns one part's arrays. A program takes and returns all parts, laid end to end along the dimension named above; each array names one. Nothing has to cross between parts.
All inputs are finite; a program needn't handle non-finite values.
Results may differ from the reference program's by a relative error of at most 0.0029.
Values may be sent and summed in bfloat16 or wider, within the bound.
No kernel may reach another device: no remote copies, remote signals or barrier semaphores. Data moves between devices by JAX's collectives and lax.ppermute only.
A program may use at most 64 MiB of HBM per device.

```python
import jax
import jax.numpy as jnp
from jax import lax

D = 256
RANK = 128
NRHS = 32
ROW_DEV = 384
ITERS = 2
LEAF = 1536
ROWS = 6144
LEVELS = 3
N_LEAF = 4
N_INNER = 4


def draw_factors(key, part):
    key = jax.random.fold_in(key, 11)
    level_ids = jnp.arange(LEVELS).astype(jnp.float32)
    scales = (LEAF * jnp.exp2(level_ids) * RANK) ** (-0.25)
    values = jax.random.normal(key, (LEVELS, ROWS, RANK), jnp.float32)
    return (values * scales[:, None, None]).astype(jnp.bfloat16)


def draw_targets(key, part):
    key = jax.random.fold_in(key, 12)
    rise = 1.0 + 2.0 * jnp.arange(ROWS).astype(jnp.float32) / ROWS
    values = jax.random.normal(key, (ROWS, NRHS), jnp.float32)
    return jnp.clip(values * rise[:, None], -12.0, 12.0)


def shard_levels(own_key, extent, split, least, high):
    factor_of = 1.0
    for position, shards_of in split:
        draws = jax.random.uniform(jax.random.fold_in(jax.random.fold_in(own_key, 6), position), (shards_of,), jnp.float32, least / len(split), high / len(split))
        factor_of = factor_of * jnp.repeat(jnp.exp(draws), extent[position] // shards_of).reshape((-1,) + (1,) * (len(extent) - 1 - position))
    return factor_of


def centred(key, shape, width, limit, cuts=(), kind=jnp.bfloat16):
    result = width * jax.random.normal(key, shape, jnp.float32)
    if cuts:
        result = result * shard_levels(key, shape, cuts, -0.22, 0.18)
    return jnp.clip(result, -limit, limit).astype(kind)


def setup_inputs(seed: int = 0, part: int = 0) -> dict:
    seeds = jax.random.split(jax.random.key(seed), 4)
    part_splits = jax.random.split(jax.random.fold_in(seeds[3], part), 4)
    embed = centred(part_splits[0], (ROWS, D), 0.25, 1.5, ((0, 16),))
    factors = draw_factors(jax.random.fold_in(jax.random.fold_in(seeds[3], part), 71), part)
    targets = draw_targets(jax.random.fold_in(jax.random.fold_in(seeds[3], part), 71), part)
    return {"embed": embed, "factors": factors, "targets": targets}


def matern(left, right):
    left_f = left.astype(jnp.float32)
    right_f = right.astype(jnp.float32)
    left_sq = lax.optimization_barrier(jnp.sum(left_f * left_f, axis=1))
    right_sq = lax.optimization_barrier(jnp.sum(right_f * right_f, axis=1))
    inner_prod = jnp.dot(left, right.T, preferred_element_type=jnp.float32)
    dist2 = left_sq[:, None] + right_sq[None, :] - 2.0 * inner_prod
    scaled = jnp.sqrt(3.0) * jnp.sqrt(jnp.maximum(dist2, 0.0)) / 2.3
    return (1.0 + scaled) * jnp.exp(-scaled)

def operate(embed, factors, field):
    leaves = embed.reshape(N_LEAF, LEAF, D)
    fields = field.reshape(N_LEAF, LEAF, NRHS)

    def one_leaf(pair):
        points, values = pair
        blocks = points.reshape(N_INNER, ROW_DEV, D)

        def one_block(block):
            return jnp.dot(matern(block, points), values, precision=lax.Precision.HIGHEST)
        return lax.map(one_block, blocks).reshape(LEAF, NRHS)
    dense = lax.map(one_leaf, (leaves, fields)).reshape(ROWS, NRHS)
    total = dense + 0.5 * field
    rounded = lax.optimization_barrier(field.astype(jnp.bfloat16)).astype(jnp.float32)
    for level in range(LEVELS):
        span = LEAF * 2 ** level
        nodes = ROWS // span
        block_factor = factors[level].reshape(nodes, span, RANK).astype(jnp.float32)
        block_field = rounded.reshape(nodes, span, NRHS)
        proj = jnp.einsum('nrk,nrc->nkc', block_factor, block_field, precision=lax.Precision.HIGHEST)
        proj_b = lax.optimization_barrier(proj.astype(jnp.bfloat16)).astype(jnp.float32)
        back = jnp.einsum('nrk,nkc->nrc', block_factor, proj_b, precision=lax.Precision.HIGHEST)
        total = total + back.reshape(ROWS, NRHS)
    return total

def reference(embed, factors, targets):
    solution = jnp.zeros_like(targets)
    residual = targets
    direction = targets
    norm_now = lax.optimization_barrier(jnp.sum(residual * residual, axis=0))
    for step in range(ITERS):
        image = operate(embed, factors, direction)
        alpha = norm_now / lax.optimization_barrier(jnp.sum(direction * image, axis=0))
        solution = solution + alpha * direction
        residual = residual - alpha * image
        if step + 1 < ITERS:
            norm_next = lax.optimization_barrier(jnp.sum(residual * residual, axis=0))
            direction = residual + norm_next / norm_now * direction
            norm_now = norm_next
    return (solution, residual)
```

```python
import functools

import jax
import jax.numpy as jnp
from jax import lax
from jax.experimental import pallas as pl
from jax.experimental.pallas import tpu as pltpu
from jax.sharding import PartitionSpec as P

ITERS = 2
LENGTH_SCALE = 2.3
FAST_LEAF = 2048
F32, BF16 = jnp.float32, jnp.bfloat16
VMEM = pl.BlockSpec(memory_space=pltpu.VMEM)
SMEM = pl.BlockSpec(memory_space=pltpu.SMEM)


def swapped(value, axis, apart):
    mask = 2**apart
    pairs = [(source, source ^ mask) for source in range(lax.axis_size(axis))]
    return lax.ppermute(value, axis, pairs)


def matern(left, right):
    left_f = left.astype(F32)
    right_f = right.astype(F32)
    left_sq = jnp.sum(left_f * left_f, axis=1)
    right_sq = jnp.sum(right_f * right_f, axis=1)
    inner_prod = lax.dot_general(
        left, right, (((1,), (1,)), ((), ())), preferred_element_type=F32
    )
    dist2 = left_sq[:, None] + right_sq[None, :] - 2.0 * inner_prod
    scaled = jnp.sqrt(3.0) * jnp.sqrt(jnp.maximum(dist2, 0.0)) / LENGTH_SCALE
    return (1.0 + scaled) * jnp.exp(-scaled)


def squares(residual):
    return lax.psum(jnp.sum(residual * residual, axis=0), ("leaf", "inner"))


def operate(embed, factors, field):
    piece = lax.all_gather(embed, "inner", axis=0, tiled=True)
    terms = jnp.dot(matern(piece, embed), field, precision=lax.Precision.HIGHEST)
    dense = lax.psum_scatter(terms, "inner", scatter_dimension=0, tiled=True)
    total = dense + 0.5 * field
    levels = factors.shape[0]
    rounded = field.astype(BF16)
    proj = jnp.einsum("lrk,rc->lkc", factors, rounded, preferred_element_type=F32)
    proj = lax.psum(proj, "inner")
    for bit in range(levels - 1):
        upper = proj[bit + 1 :]
        partner = swapped(upper, "leaf", bit)
        proj = jnp.concatenate([proj[: bit + 1], upper + partner], axis=0)
    back = jnp.einsum(
        "lrk,lkc->rc", factors, proj.astype(BF16), preferred_element_type=F32
    )
    return total + back


def stepwise(embed, factors, targets):
    result = jnp.zeros_like(targets)
    residual = targets
    direction = targets
    norm_now = squares(residual)
    for step in range(ITERS):
        image = operate(embed, factors, direction)
        curv = lax.psum(jnp.sum(direction * image, axis=0), ("leaf", "inner"))
        alpha = norm_now / curv
        result = result + alpha * direction
        residual = residual - alpha * image
        if step + 1 < ITERS:
            norm_next = squares(residual)
            direction = residual + norm_next / norm_now * direction
            norm_now = norm_next
    return (result, residual)


def mm(left, right):
    return lax.dot_general(left, right, (((1,), (0,)), ((), ())), preferred_element_type=F32)


def mm_nt(left, right):
    return lax.dot_general(left, right, (((1,), (1,)), ((), ())), preferred_element_type=F32)


def pairs_of(slots):
    return [(i, j) for j in range(slots) for i in range(j + 1)]


def wide(pieces, nrhs):
    count = pieces.shape[0] // nrhs
    return jnp.concatenate([pieces[k * nrhs : (k + 1) * nrhs] for k in range(count)], axis=1)


def project_kernel(factors_ref, field_ref, proj_ref):
    levels = factors_ref.shape[0]
    nrhs = field_ref.shape[0]
    rounded = field_ref[...].astype(BF16)
    for level in range(levels):
        proj_ref[level * nrhs : (level + 1) * nrhs] = mm(rounded, factors_ref[level])


def pack_kernel(starts, field_ref, proj_ref, *refs):
    out_ref = refs[-1]
    nrhs = field_ref.shape[0]
    width = proj_ref.shape[1]
    count = field_ref.shape[1] // width
    for k in range(count):
        out_ref[k * nrhs : (k + 1) * nrhs] = field_ref[:, k * width : (k + 1) * width]
    base = count * nrhs
    levels = proj_ref.shape[0] // nrhs
    for level in range(levels):
        total = proj_ref[level * nrhs : (level + 1) * nrhs]
        for start, ref in zip(starts, refs[:-1]):
            if level >= start:
                total = total + ref[(level - start) * nrhs : (level - start + 1) * nrhs]
        out_ref[base + level * nrhs : base + (level + 1) * nrhs] = total


def kern_kernel(slots, *refs):
    embeds = refs[:slots]
    high_ref, low_ref, column_ref, row_ref = refs[slots:]
    rows, dims = embeds[0].shape
    scale = 3.0 / LENGTH_SCALE**2
    ones = jnp.ones((8, dims), BF16)
    for s in range(slots):
        wide_e = embeds[s][...].astype(F32)
        square = wide_e * wide_e
        column_ref[s] = jnp.broadcast_to(
            scale * jnp.sum(square, axis=1, keepdims=True), (rows, 128)
        )
        first = square.astype(BF16)
        rest = (square - first.astype(F32)).astype(BF16)
        row_ref[s] = scale * (mm_nt(ones, first) + mm_nt(ones, rest))
    chunk = 128
    for index, (i, j) in enumerate(pairs_of(slots)):
        right = embeds[j][...]
        row = row_ref[j, 0:1]

        def part(c, carry, i=i, index=index, right=right, row=row):
            span = pl.ds(pl.multiple_of(c * chunk, chunk), chunk)
            product = mm_nt(embeds[i][span], right)
            column = column_ref[i, span, 0:1]
            dist = jnp.maximum((column + row) - (2.0 * scale) * product, 1e-30)
            scaled = dist * lax.rsqrt(dist)
            value = (1.0 + scaled) * jnp.exp(-scaled)
            high = value.astype(BF16)
            high_ref[index, span] = high
            low_ref[index, span] = (value - high.astype(F32)).astype(BF16)
            return carry

        lax.fori_loop(0, rows // chunk, part, 0)


def main_kernel(slots, is_host_ref, high_ref, low_ref, *refs):
    factors = refs[:slots]
    packs = refs[slots : 2 * slots]
    sums_ref = refs[2 * slots]
    fields_out = refs[2 * slots + 1 :]
    levels, rows, rank = factors[0].shape
    nrhs = packs[0].shape[0] // (rows // rank + levels)
    lead = rows // rank * nrhs
    pairs = pairs_of(slots)
    field = [wide(packs[s][:lead], nrhs) for s in range(slots)]
    proj = packs[0][lead:]
    for s in range(1, slots):
        proj = proj + packs[s][lead:]
    proj = proj.astype(BF16)
    first = [f.astype(BF16) for f in field]
    both = [
        jnp.concatenate([h, (f - h.astype(F32)).astype(BF16)], axis=0)
        for f, h in zip(field, first)
    ]
    image = []
    for s in range(slots):
        total = 0.5 * field[s]
        for level in range(levels):
            total = total + mm_nt(proj[level * nrhs : (level + 1) * nrhs], factors[s][level])
        image.append(total)

    def add(total, stacked, second):
        return total + (stacked[:nrhs] + stacked[nrhs:] + second)

    for index, (i, j) in enumerate(pairs):
        high, low = high_ref[index], low_ref[index]
        image[j] = add(image[j], mm(both[i], high), mm(first[i], low))
        if i != j:
            image[i] = add(image[i], mm_nt(both[j], high), mm_nt(first[j], low))
    mine = is_host_ref[0] == 1

    def own(value, s):
        return jnp.where(mine, value, jnp.zeros_like(value)) if s == 0 else value

    image_b = []
    for s in range(slots):
        high = image[s].astype(BF16)
        image_b.append(high)
        fields_out[s][:nrhs] = own(image[s], s)
    norms = []
    for level in range(levels):
        total = mm(image_b[0], factors[0][level])
        for s in range(1, slots):
            total = total + mm(image_b[s], factors[s][level])
        if level == 0:
            norms.append(jnp.sum(total * total, axis=1, keepdims=True))
        sums_ref[:, level * rank : (level + 1) * rank] = own(total.astype(BF16), 0)
    second = [jnp.zeros((nrhs, rows), F32) for _ in range(slots)]
    for index, (i, j) in enumerate(pairs):
        high = high_ref[index]
        second[j] = second[j] + mm(image_b[i], high)
        if i != j:
            second[i] = second[i] + mm_nt(image_b[j], high)
    for s in range(slots):
        fields_out[s][nrhs:] = own(second[s], s)

    def dots(left, right):
        total = left[0] * right[0]
        for s in range(1, slots):
            total = total + left[s] * right[s]
        return jnp.sum(total, axis=1, keepdims=True)

    scalars = [
        dots(field, field),
        dots(field, image),
        dots(image, image),
        dots(image, second) + norms[0],
    ]
    lane = lax.broadcasted_iota(jnp.int32, (nrhs, 128), 1)
    packed = jnp.zeros((nrhs, 128), F32)
    for k, value in enumerate(scalars):
        value = jnp.broadcast_to(value, (nrhs, 128))
        for piece in range(3):
            rounded = value.astype(BF16).astype(F32)
            packed = jnp.where(lane == 3 * k + piece, rounded, packed)
            value = value - rounded
    sums_ref[:, levels * rank :] = own(packed.astype(BF16), 0)


def finish_kernel(leaves, slots, field_ref, factors_ref, *refs):
    sums = refs[:leaves]
    parts = refs[leaves : leaves + slots]
    solution_ref, residual_ref = refs[leaves + slots :]
    levels, rows, rank = factors_ref.shape
    nrhs = field_ref.shape[0]
    field = field_ref[...]
    total = parts[0][...]
    for s in range(1, slots):
        total = total + parts[s][...]
    image = total[:nrhs]
    second = total[nrhs:] + 0.5 * image
    lane = lax.broadcasted_iota(jnp.int32, (nrhs, 128), 1)
    packed = sums[0][:, levels * rank :].astype(F32)
    for m in range(1, leaves):
        packed = packed + sums[m][:, levels * rank :].astype(F32)

    def scalar(k):
        inside = (lane >= 3 * k) & (lane < 3 * k + 3)
        return jnp.sum(jnp.where(inside, packed, 0.0), axis=1, keepdims=True)

    bb, bw, ww, wu = (scalar(k) for k in range(4))
    wu = wu + 0.5 * ww
    for level in range(levels):
        nodes = {}
        for m in range(leaves):
            value = sums[m][:, level * rank : (level + 1) * rank].astype(F32)
            node = m >> level
            nodes[node] = nodes[node] + value if node in nodes else value
        second = second + mm_nt(nodes[0].astype(BF16), factors_ref[level])
        if level > 0:
            squared = sum(value * value for value in nodes.values())
            wu = wu + jnp.sum(squared, axis=1, keepdims=True)
    alpha0 = bb / bw
    norm1 = alpha0 * alpha0 * ww - bb
    ratio = norm1 / bb
    keep = 1.0 + ratio
    curv = keep * keep * bw - 2.0 * keep * alpha0 * ww + alpha0 * alpha0 * wu
    alpha1 = norm1 / curv
    solution_ref[...] = (alpha0 + alpha1 * keep) * field - (alpha1 * alpha0) * image
    residual_ref[...] = field - (alpha0 + alpha1 * keep) * image + (alpha1 * alpha0) * second


def call(kernel, outs, args, in_smem=0, scratch=(), flops=0, limit=24):
    moved = sum(a.size * a.dtype.itemsize for a in args)
    return pl.pallas_call(
        kernel,
        out_shape=[jax.ShapeDtypeStruct(shape, dtype) for shape, dtype in outs],
        in_specs=[SMEM] * in_smem + [VMEM] * (len(args) - in_smem),
        out_specs=[VMEM] * len(outs),
        scratch_shapes=list(scratch),
        cost_estimate=pl.CostEstimate(flops=flops, bytes_accessed=moved, transcendentals=0),
        compiler_params=pltpu.CompilerParams(vmem_limit_bytes=limit * 2**20),
    )(*args)


def collected(embed, factors, targets):
    leaves, inner = lax.axis_size("leaf"), lax.axis_size("inner")
    levels, rows, rank = factors.shape
    nrhs = targets.shape[1]

    def host(leaf):
        return inner // 2 if leaf % 2 == 0 else (inner - 1) // 2

    def others(leaf):
        sign = 1 if leaf % 2 == 0 else -1
        here = host(leaf)
        return sorted((z for z in range(inner) if z != here), key=lambda z: (abs(z - here), sign * z))

    routes = [
        [(leaf * inner + others(leaf)[k], leaf * inner + host(leaf)) for leaf in range(leaves)]
        for k in range(inner - 1)
    ]

    def to_host(value):
        return [value] + [lax.ppermute(value, ("leaf", "inner"), route) for route in routes]

    def from_host(values):
        back = [
            lax.ppermute(value, ("leaf", "inner"), [(b, a) for a, b in route])
            for value, route in zip(values[1:], routes)
        ]
        return [values[0]] + back

    def over_leaf(value, m):
        return lax.ppermute(value, "leaf", [(i, i ^ m) for i in range(leaves)])

    field = targets.T
    embeds = to_host(embed)
    factor_slots = to_host(factors)
    (proj,) = call(project_kernel, [((levels * nrhs, rank), F32)], [factors, field])
    starts, arrived = [], []
    for m in range(1, leaves):
        start = m.bit_length()
        if start < levels:
            starts.append(start)
            arrived.append(over_leaf(proj[start * nrhs :], m))
    height = rows // rank * nrhs + levels * nrhs
    (pack,) = call(
        functools.partial(pack_kernel, starts), [((height, rank), F32)], [field, proj] + arrived
    )
    packs = to_host(pack)
    pairs = len(pairs_of(inner))
    high, low = call(
        functools.partial(kern_kernel, inner),
        [((pairs, rows, rows), BF16)] * 2,
        embeds,
        scratch=[pltpu.VMEM((inner, rows, 128), F32), pltpu.VMEM((inner, 8, rows), F32)],
        flops=2 * pairs * rows * rows * embed.shape[1],
    )
    leaf = lax.axis_index("leaf")
    here = jnp.where(leaf % 2 == 0, host(0), host(1))
    is_host = (lax.axis_index("inner") == here).astype(jnp.int32).reshape(1)
    results = call(
        functools.partial(main_kernel, inner),
        [((nrhs, levels * rank + 128), BF16)] + [((2 * nrhs, rows), F32)] * inner,
        [is_host, high, low] + factor_slots + packs,
        in_smem=1,
    )
    sums = sum(from_host([results[0]] * inner))
    parts = from_host(results[1:])
    leaf_sums = [sums] + [over_leaf(sums, m) for m in range(1, leaves)]
    result, residual = call(
        functools.partial(finish_kernel, leaves, inner),
        [((nrhs, rows), F32)] * 2,
        [field, factors] + leaf_sums + parts,
    )
    return (result.T, residual.T)


def on_device(embed, factors, targets):
    if embed.shape[0] * lax.axis_size("inner") <= FAST_LEAF:
        return collected(embed, factors, targets)
    return stepwise(embed, factors, targets)


def solution(mesh):
    return jax.shard_map(
        on_device,
        mesh=mesh,
        in_specs=(
            P(("groups", "leaf", "inner"), None),
            P(None, ("groups", "leaf", "inner"), None),
            P(("groups", "leaf", "inner"), None),
        ),
        out_specs=(P(("groups", "leaf", "inner"), None), P(("groups", "leaf", "inner"), None)),
        check_vma=False,
    )
```

```python
import functools

import jax
import jax.numpy as jnp
from jax import lax
from jax.experimental import pallas as pl
from jax.experimental.pallas import tpu as pltpu
from jax.sharding import PartitionSpec as P

ITERS = 2
LENGTH_SCALE = 2.3
FAST_LEAF = 2048
NEAR_FLOPS = 2 * 10**9
MAIN_FLOPS = 4 * 10**9
F32, BF16 = jnp.float32, jnp.bfloat16
VMEM = pl.BlockSpec(memory_space=pltpu.VMEM)
SMEM = pl.BlockSpec(memory_space=pltpu.SMEM)


def swapped(value, axis, apart):
    mask = 2**apart
    pairs = [(source, source ^ mask) for source in range(lax.axis_size(axis))]
    return lax.ppermute(value, axis, pairs)


def matern(left, right):
    left_f = left.astype(F32)
    right_f = right.astype(F32)
    left_sq = jnp.sum(left_f * left_f, axis=1)
    right_sq = jnp.sum(right_f * right_f, axis=1)
    inner_prod = lax.dot_general(
        left, right, (((1,), (1,)), ((), ())), preferred_element_type=F32
    )
    dist2 = left_sq[:, None] + right_sq[None, :] - 2.0 * inner_prod
    scaled = jnp.sqrt(3.0) * jnp.sqrt(jnp.maximum(dist2, 0.0)) / LENGTH_SCALE
    return (1.0 + scaled) * jnp.exp(-scaled)


def squares(residual):
    return lax.psum(jnp.sum(residual * residual, axis=0), ("leaf", "inner"))


def operate(embed, factors, field):
    piece = lax.all_gather(embed, "inner", axis=0, tiled=True)
    terms = jnp.dot(matern(piece, embed), field, precision=lax.Precision.HIGHEST)
    dense = lax.psum_scatter(terms, "inner", scatter_dimension=0, tiled=True)
    total = dense + 0.5 * field
    levels = factors.shape[0]
    rounded = field.astype(BF16)
    proj = jnp.einsum("lrk,rc->lkc", factors, rounded, preferred_element_type=F32)
    proj = lax.psum(proj, "inner")
    for bit in range(levels - 1):
        upper = proj[bit + 1 :]
        partner = swapped(upper, "leaf", bit)
        proj = jnp.concatenate([proj[: bit + 1], upper + partner], axis=0)
    back = jnp.einsum(
        "lrk,lkc->rc", factors, proj.astype(BF16), preferred_element_type=F32
    )
    return total + back


def stepwise(embed, factors, targets):
    result = jnp.zeros_like(targets)
    residual = targets
    direction = targets
    norm_now = squares(residual)
    for step in range(ITERS):
        image = operate(embed, factors, direction)
        curv = lax.psum(jnp.sum(direction * image, axis=0), ("leaf", "inner"))
        alpha = norm_now / curv
        result = result + alpha * direction
        residual = residual - alpha * image
        if step + 1 < ITERS:
            norm_next = squares(residual)
            direction = residual + norm_next / norm_now * direction
            norm_now = norm_next
    return (result, residual)


def mm(left, right):
    return lax.dot_general(left, right, (((1,), (0,)), ((), ())), preferred_element_type=F32)


def mm_nt(left, right):
    return lax.dot_general(left, right, (((1,), (1,)), ((), ())), preferred_element_type=F32)


def pairs_of(slots):
    return [(i, j) for j in range(slots) for i in range(j + 1)]


def pack_kernel(embed_hbm, factors_hbm, field_hbm, message_ref, proj_ref, field_ref, sems):
    levels, rows, rank = factors_hbm.shape
    nrhs = field_ref.shape[0]
    lanes = embed_hbm.shape[1] // rank
    copies = [
        pltpu.make_async_copy(field_hbm, field_ref, sems.at[0]),
    ]
    for level in range(levels):
        place = message_ref.at[pl.ds((lanes + level) * rows, rows)]
        copies.append(pltpu.make_async_copy(factors_hbm.at[level], place, sems.at[1 + level]))
    for k in range(lanes):
        piece = embed_hbm.at[:, pl.ds(k * rank, rank)]
        place = message_ref.at[pl.ds(k * rows, rows)]
        copies.append(pltpu.make_async_copy(piece, place, sems.at[1 + levels + k]))
    for copy in copies:
        copy.start()
    copies[0].wait()
    field = field_ref[...]
    high = field.astype(BF16)
    low = (field - high.astype(F32)).astype(BF16)
    base = (lanes + levels) * rows
    for k in range(rows // rank):
        span = slice(k * rank, (k + 1) * rank)
        message_ref[base + 2 * k * nrhs : base + (2 * k + 1) * nrhs] = high[:, span]
        message_ref[base + (2 * k + 1) * nrhs : base + (2 * k + 2) * nrhs] = low[:, span]
    for level in range(levels):
        copies[1 + level].wait()
        factor = message_ref[(lanes + level) * rows : (lanes + level + 1) * rows]
        proj_ref[level * nrhs : (level + 1) * nrhs] = mm(high, factor)
    for k in range(lanes):
        copies[1 + levels + k].wait()


class Message:
    def __init__(self, ref, shape):
        self.ref = ref
        self.rows, self.dims, self.levels, self.rank, self.nrhs = shape
        self.lanes = self.dims // self.rank

    def embed(self):
        rows = self.rows
        return jnp.concatenate(
            [self.ref[k * rows : (k + 1) * rows] for k in range(self.lanes)], axis=1
        )

    def factor(self, level):
        start = (self.lanes + level) * self.rows
        return self.ref[start : start + self.rows]

    def field(self):
        base = (self.lanes + self.levels) * self.rows
        step = 2 * self.nrhs
        return jnp.concatenate(
            [self.ref[base + k * step : base + (k + 1) * step] for k in range(self.rows // self.rank)],
            axis=1,
        )


def norms_of(embed):
    scale = 3.0 / LENGTH_SCALE**2
    wide_e = embed.astype(F32)
    square = wide_e * wide_e
    column = scale * jnp.sum(square, axis=1, keepdims=True)
    first = square.astype(BF16)
    rest = (square - first.astype(F32)).astype(BF16)
    ones = jnp.ones((8, embed.shape[1]), BF16)
    row = scale * (mm_nt(ones, first) + mm_nt(ones, rest))
    return column, row[0:1]


def kern_block(left, right, column, row):
    scale = 3.0 / LENGTH_SCALE**2
    product = mm_nt(left, right)
    dist = jnp.maximum((column + row) - (2.0 * scale) * product, 1e-30)
    scaled = dist * lax.rsqrt(dist)
    value = (1.0 + scaled) * jnp.exp(-scaled)
    high = value.astype(BF16)
    return high, (value - high.astype(F32)).astype(BF16)


def first_products(pairs, messages, high_ref, image_ref):
    nrhs = messages[0].nrhs
    norms = {}
    for index, (i, j) in enumerate(pairs):
        for s in (i, j):
            if s not in norms:
                norms[s] = norms_of(messages[s].embed())
        high, low = kern_block(messages[i].embed(), messages[j].embed(), norms[i][0], norms[j][1])
        high_ref[index] = high
        field = messages[i].field()
        stacked = mm(field, high)
        image_ref[j] += stacked[:nrhs] + stacked[nrhs:] + mm(field[:nrhs], low)
        if i != j:
            field = messages[j].field()
            stacked = mm_nt(field, high)
            image_ref[i] += stacked[:nrhs] + stacked[nrhs:] + mm_nt(field[:nrhs], low)


def near_kernel(near, shape, *refs):
    high_ref, image_ref = refs[near:]
    image_ref[...] = jnp.zeros_like(image_ref)
    messages = [Message(ref, shape) for ref in refs[:near]]
    first_products(pairs_of(near), messages, high_ref, image_ref)


def main_kernel(slots, shape, is_host_ref, near_high_ref, near_image_ref, *refs):
    messages = [Message(ref, shape) for ref in refs[:slots]]
    sums_in = refs[slots : 2 * slots]
    sums_ref = refs[2 * slots]
    fields_out = refs[2 * slots + 1 : -2]
    far_high_ref, image_ref = refs[-2:]
    rows, _, levels, rank, nrhs = shape
    near = near_image_ref.shape[0]
    pairs = pairs_of(slots)
    held = len(pairs_of(near))
    image_ref[:near] = near_image_ref[...]
    image_ref[near:] = jnp.zeros_like(image_ref[near:])
    first_products(pairs[held:], messages, far_high_ref, image_ref)
    proj = sums_in[0][...]
    for s in range(1, slots):
        proj = proj + sums_in[s][...]
    proj = proj.astype(BF16)
    mine = is_host_ref[0] == 1

    def own(value, s):
        return jnp.where(mine, value, jnp.zeros_like(value)) if s == 0 else value

    field, image, image_b = [], [], []
    for s in range(slots):
        halves = messages[s].field().astype(F32)
        field.append(halves[:nrhs] + halves[nrhs:])
        total = image_ref[s] + 0.5 * field[s]
        for level in range(levels):
            total = total + mm_nt(proj[level * nrhs : (level + 1) * nrhs], messages[s].factor(level))
        image.append(total)
        image_b.append(total.astype(BF16))
        fields_out[s][:nrhs] = own(total, s)
    norms = []
    for level in range(levels):
        total = mm(image_b[0], messages[0].factor(level))
        for s in range(1, slots):
            total = total + mm(image_b[s], messages[s].factor(level))
        if level == 0:
            norms.append(jnp.sum(total * total, axis=1, keepdims=True))
        sums_ref[:, level * rank : (level + 1) * rank] = own(total.astype(BF16), 0)
    second = [jnp.zeros((nrhs, rows), F32) for _ in range(slots)]
    for index, (i, j) in enumerate(pairs):
        high = near_high_ref[index] if index < held else far_high_ref[index - held]
        second[j] = second[j] + mm(image_b[i], high)
        if i != j:
            second[i] = second[i] + mm_nt(image_b[j], high)
    for s in range(slots):
        fields_out[s][nrhs:] = own(second[s], s)

    def dots(left, right):
        total = left[0] * right[0]
        for s in range(1, slots):
            total = total + left[s] * right[s]
        return jnp.sum(total, axis=1, keepdims=True)

    scalars = [
        dots(field, field),
        dots(field, image),
        dots(image, image),
        dots(image, second) + norms[0],
    ]
    lane = lax.broadcasted_iota(jnp.int32, (nrhs, 128), 1)
    packed = jnp.zeros((nrhs, 128), F32)
    for k, value in enumerate(scalars):
        value = jnp.broadcast_to(value, (nrhs, 128))
        for piece in range(3):
            rounded = value.astype(BF16).astype(F32)
            packed = jnp.where(lane == 3 * k + piece, rounded, packed)
            value = value - rounded
    sums_ref[:, levels * rank :] = own(packed.astype(BF16), 0)


def finish_kernel(leaves, slots, shape, field_ref, message_ref, *refs):
    sums = refs[:leaves]
    parts = refs[leaves : leaves + slots]
    solution_ref, residual_ref = refs[leaves + slots :]
    rows, _, levels, rank, nrhs = shape
    message = Message(message_ref, shape)
    field = field_ref[...]
    total = parts[0][...]
    for s in range(1, slots):
        total = total + parts[s][...]
    image = total[:nrhs]
    second = total[nrhs:] + 0.5 * image
    lane = lax.broadcasted_iota(jnp.int32, (nrhs, 128), 1)
    packed = sums[0][:, levels * rank :].astype(F32)
    for m in range(1, leaves):
        packed = packed + sums[m][:, levels * rank :].astype(F32)

    def scalar(k):
        inside = (lane >= 3 * k) & (lane < 3 * k + 3)
        return jnp.sum(jnp.where(inside, packed, 0.0), axis=1, keepdims=True)

    bb, bw, ww, wu = (scalar(k) for k in range(4))
    wu = wu + 0.5 * ww
    for level in range(levels):
        nodes = {}
        for m in range(leaves):
            value = sums[m][:, level * rank : (level + 1) * rank].astype(F32)
            node = m >> level
            nodes[node] = nodes[node] + value if node in nodes else value
        second = second + mm_nt(nodes[0].astype(BF16), message.factor(level))
        if level > 0:
            squared = sum(value * value for value in nodes.values())
            wu = wu + jnp.sum(squared, axis=1, keepdims=True)
    alpha0 = bb / bw
    norm1 = alpha0 * alpha0 * ww - bb
    ratio = norm1 / bb
    keep = 1.0 + ratio
    curv = keep * keep * bw - 2.0 * keep * alpha0 * ww + alpha0 * alpha0 * wu
    alpha1 = norm1 / curv
    solution_ref[...] = (alpha0 + alpha1 * keep) * field - (alpha1 * alpha0) * image
    residual_ref[...] = field - (alpha0 + alpha1 * keep) * image + (alpha1 * alpha0) * second


def call(kernel, outs, args, specs, scratch=(), flops=0, limit=24):
    moved = sum(a.size * a.dtype.itemsize for a in args)
    return pl.pallas_call(
        kernel,
        out_shape=[jax.ShapeDtypeStruct(shape, dtype) for shape, dtype in outs],
        in_specs=specs,
        out_specs=[VMEM] * len(outs),
        scratch_shapes=list(scratch),
        cost_estimate=pl.CostEstimate(flops=flops, bytes_accessed=moved, transcendentals=0),
        compiler_params=pltpu.CompilerParams(vmem_limit_bytes=limit * 2**20),
    )(*args)


def collected(embed, factors, targets):
    leaves, inner = lax.axis_size("leaf"), lax.axis_size("inner")
    levels, rows, rank = factors.shape
    dims, nrhs = embed.shape[1], targets.shape[1]
    shape = (rows, dims, levels, rank, nrhs)

    def host(leaf):
        return inner // 2 if leaf % 2 == 0 else (inner - 1) // 2

    def others(leaf):
        sign = 1 if leaf % 2 == 0 else -1
        here = host(leaf)
        return sorted((z for z in range(inner) if z != here), key=lambda z: (abs(z - here), sign * z))

    routes = [
        [(leaf * inner + others(leaf)[k], leaf * inner + host(leaf)) for leaf in range(leaves)]
        for k in range(inner - 1)
    ]

    def to_host(value):
        return [value] + [lax.ppermute(value, ("leaf", "inner"), route) for route in routes]

    def from_host(values):
        back = [
            lax.ppermute(value, ("leaf", "inner"), [(b, a) for a, b in route])
            for value, route in zip(values[1:], routes)
        ]
        return [values[0]] + back

    def over_leaf(value, m):
        return lax.ppermute(value, "leaf", [(i, i ^ m) for i in range(leaves)])

    height = (dims // rank + levels) * rows + 2 * nrhs * (rows // rank)
    message, proj, field = call(
        pack_kernel,
        [((height, rank), BF16), ((levels * nrhs, rank), F32), ((nrhs, rows), F32)],
        [embed, factors, targets.T],
        [pl.BlockSpec(memory_space=pltpu.HBM)] * 3,
        scratch=[pltpu.SemaphoreType.DMA((1 + levels + dims // rank,))],
    )
    messages = to_host(message)
    pieces = [proj[level * nrhs : (level + 1) * nrhs] for level in range(levels)]
    for m in range(1, leaves):
        start = m.bit_length()
        if start < levels:
            arrived = over_leaf(proj[start * nrhs :], m)
            for level in range(start, levels):
                at = (level - start) * nrhs
                pieces[level] = pieces[level] + arrived[at : at + nrhs]
    near = inner - 1
    held = len(pairs_of(near))
    near_high, near_image = call(
        functools.partial(near_kernel, near, shape),
        [((held, rows, rows), BF16), ((near, nrhs, rows), F32)],
        messages[:near],
        [VMEM] * near,
        flops=NEAR_FLOPS,
    )
    partial_sums = to_host(jnp.concatenate(pieces, axis=0))
    leaf = lax.axis_index("leaf")
    here = jnp.where(leaf % 2 == 0, host(0), host(1))
    is_host = (lax.axis_index("inner") == here).astype(jnp.int32).reshape(1)
    results = call(
        functools.partial(main_kernel, inner, shape),
        [((nrhs, levels * rank + 128), BF16)] + [((2 * nrhs, rows), F32)] * inner,
        [is_host, near_high, near_image] + messages + partial_sums,
        [SMEM] + [VMEM] * (2 + 2 * inner),
        scratch=[
            pltpu.VMEM((len(pairs_of(inner)) - held, rows, rows), BF16),
            pltpu.VMEM((inner, nrhs, rows), F32),
        ],
        flops=MAIN_FLOPS,
    )
    sums = sum(from_host([results[0]] * inner))
    parts = from_host(results[1:])
    leaf_sums = [sums] + [over_leaf(sums, m) for m in range(1, leaves)]
    result, residual = call(
        functools.partial(finish_kernel, leaves, inner, shape),
        [((nrhs, rows), F32)] * 2,
        [field, message] + leaf_sums + parts,
        [VMEM] * (2 + leaves + inner),
    )
    return (result.T, residual.T)


def on_device(embed, factors, targets):
    if embed.shape[0] * lax.axis_size("inner") <= FAST_LEAF:
        return collected(embed, factors, targets)
    return stepwise(embed, factors, targets)


def solution(mesh):
    return jax.shard_map(
        on_device,
        mesh=mesh,
        in_specs=(
            P(("groups", "leaf", "inner"), None),
            P(None, ("groups", "leaf", "inner"), None),
            P(("groups", "leaf", "inner"), None),
        ),
        out_specs=(P(("groups", "leaf", "inner"), None), P(("groups", "leaf", "inner"), None)),
        check_vma=False,
    )
```

```python
import functools

import jax
import jax.numpy as jnp
from jax import lax
from jax.experimental import pallas as pl
from jax.experimental.pallas import tpu as pltpu
from jax.sharding import PartitionSpec as P

ITERS = 2
LENGTH_SCALE = 2.3
FAST_LEAF = 2048
NEAR_FLOPS = 4 * 10**9
FAR_FLOPS = 3 * 10**9
MAIN_FLOPS = 2 * 10**9
F32, BF16 = jnp.float32, jnp.bfloat16
VMEM = pl.BlockSpec(memory_space=pltpu.VMEM)
SMEM = pl.BlockSpec(memory_space=pltpu.SMEM)


def swapped(value, axis, apart):
    mask = 2**apart
    pairs = [(source, source ^ mask) for source in range(lax.axis_size(axis))]
    return lax.ppermute(value, axis, pairs)


def matern(left, right):
    left_f = left.astype(F32)
    right_f = right.astype(F32)
    left_sq = jnp.sum(left_f * left_f, axis=1)
    right_sq = jnp.sum(right_f * right_f, axis=1)
    inner_prod = lax.dot_general(
        left, right, (((1,), (1,)), ((), ())), preferred_element_type=F32
    )
    dist2 = left_sq[:, None] + right_sq[None, :] - 2.0 * inner_prod
    scaled = jnp.sqrt(3.0) * jnp.sqrt(jnp.maximum(dist2, 0.0)) / LENGTH_SCALE
    return (1.0 + scaled) * jnp.exp(-scaled)


def squares(residual):
    return lax.psum(jnp.sum(residual * residual, axis=0), ("leaf", "inner"))


def operate(embed, factors, field):
    piece = lax.all_gather(embed, "inner", axis=0, tiled=True)
    terms = jnp.dot(matern(piece, embed), field, precision=lax.Precision.HIGHEST)
    dense = lax.psum_scatter(terms, "inner", scatter_dimension=0, tiled=True)
    total = dense + 0.5 * field
    levels = factors.shape[0]
    rounded = field.astype(BF16)
    proj = jnp.einsum("lrk,rc->lkc", factors, rounded, preferred_element_type=F32)
    proj = lax.psum(proj, "inner")
    for bit in range(levels - 1):
        upper = proj[bit + 1 :]
        partner = swapped(upper, "leaf", bit)
        proj = jnp.concatenate([proj[: bit + 1], upper + partner], axis=0)
    back = jnp.einsum(
        "lrk,lkc->rc", factors, proj.astype(BF16), preferred_element_type=F32
    )
    return total + back


def stepwise(embed, factors, targets):
    result = jnp.zeros_like(targets)
    residual = targets
    direction = targets
    norm_now = squares(residual)
    for step in range(ITERS):
        image = operate(embed, factors, direction)
        curv = lax.psum(jnp.sum(direction * image, axis=0), ("leaf", "inner"))
        alpha = norm_now / curv
        result = result + alpha * direction
        residual = residual - alpha * image
        if step + 1 < ITERS:
            norm_next = squares(residual)
            direction = residual + norm_next / norm_now * direction
            norm_now = norm_next
    return (result, residual)


def mm(left, right):
    return lax.dot_general(left, right, (((1,), (0,)), ((), ())), preferred_element_type=F32)


def mm_nt(left, right):
    return lax.dot_general(left, right, (((1,), (1,)), ((), ())), preferred_element_type=F32)


def pairs_of(slots):
    return [(i, j) for j in range(slots) for i in range(j + 1)]


def project_kernel(factors_ref, field_ref, first_ref, upper_ref):
    levels = factors_ref.shape[0]
    nrhs = field_ref.shape[0]
    rounded = field_ref[...].astype(BF16)
    first_ref[...] = mm(rounded, factors_ref[0])
    for level in range(1, levels):
        upper_ref[(level - 1) * nrhs : level * nrhs] = mm(rounded, factors_ref[level])


def pack_kernel(embed_hbm, factors_hbm, field_hbm, message_ref, field_ref, sems):
    levels, rows, rank = factors_hbm.shape
    nrhs = field_ref.shape[0]
    lanes = embed_hbm.shape[1] // rank
    head = lanes * rows + 2 * nrhs * (rows // rank)
    copies = [pltpu.make_async_copy(field_hbm, field_ref, sems.at[0])]
    for k in range(lanes):
        piece = embed_hbm.at[:, pl.ds(k * rank, rank)]
        place = message_ref.at[pl.ds(k * rows, rows)]
        copies.append(pltpu.make_async_copy(piece, place, sems.at[len(copies)]))
    for level in range(levels):
        place = message_ref.at[pl.ds(head + level * rows, rows)]
        copies.append(pltpu.make_async_copy(factors_hbm.at[level], place, sems.at[len(copies)]))
    for copy in copies:
        copy.start()
    copies[0].wait()
    for k in range(rows // rank):
        start = lanes * rows + 2 * k * nrhs
        value = field_ref[:, k * rank : (k + 1) * rank]
        high = value.astype(BF16)
        message_ref[start : start + nrhs] = high
        message_ref[start + nrhs : start + 2 * nrhs] = (value - high.astype(F32)).astype(BF16)
    for copy in copies[1:]:
        copy.wait()


class Message:
    def __init__(self, shape, ref):
        self.rows, self.dims, self.levels, self.rank, self.nrhs = shape
        self.ref = ref

    def embed(self):
        rows = self.rows
        pieces = [self.ref[k * rows : (k + 1) * rows] for k in range(self.dims // self.rank)]
        return jnp.concatenate(pieces, axis=1)

    def field(self):
        base = self.dims // self.rank * self.rows
        step = 2 * self.nrhs
        count = self.rows // self.rank
        pieces = [self.ref[base + k * step : base + (k + 1) * step] for k in range(count)]
        return jnp.concatenate(pieces, axis=1)

    def factor(self, level):
        base = self.dims // self.rank * self.rows + 2 * self.nrhs * (self.rows // self.rank)
        return self.ref[base + level * self.rows : base + (level + 1) * self.rows]

    def project(self, field):
        return jnp.concatenate([mm(field, self.factor(l)) for l in range(self.levels)], axis=0)


def norms_of(embed):
    scale = 3.0 / LENGTH_SCALE**2
    wide_e = embed.astype(F32)
    square = wide_e * wide_e
    column = scale * jnp.sum(square, axis=1, keepdims=True)
    first = square.astype(BF16)
    rest = (square - first.astype(F32)).astype(BF16)
    ones = jnp.ones((8, embed.shape[1]), BF16)
    row = scale * (mm_nt(ones, first) + mm_nt(ones, rest))
    return column, row[0:1]


def kern_block(left, right, column, row):
    scale = 3.0 / LENGTH_SCALE**2
    product = mm_nt(left, right)
    dist = jnp.maximum((column + row) - (2.0 * scale) * product, 1e-30)
    scaled = dist * lax.rsqrt(dist)
    value = (1.0 + scaled) * jnp.exp(-scaled)
    high = value.astype(BF16)
    return high, (value - high.astype(F32)).astype(BF16)


def kern_columns(columns, messages, high_ref, low_ref):
    norms = {}
    index = 0
    for j in columns:
        for i in range(j + 1):
            for s in (i, j):
                if s not in norms:
                    norms[s] = norms_of(messages[s].embed())
            high_ref[index], low_ref[index] = kern_block(
                messages[i].embed(), messages[j].embed(), norms[i][0], norms[j][1]
            )
            index += 1


def add_products(columns, high_ref, low_ref, fields, total):
    nrhs, rows = total[0].shape

    def fold(stacked):
        return stacked[:nrhs] + stacked[nrhs:] if stacked.shape[0] > nrhs else stacked

    at = 0
    for j in columns:
        left = jnp.concatenate(fields[: j + 1], axis=1)
        high = high_ref[at : at + j + 1].reshape((j + 1) * rows, rows)
        down = fold(mm(left, high))
        across = fold(mm_nt(fields[j], high[: j * rows])) if j else None
        if low_ref is not None:
            low = low_ref[at : at + j + 1].reshape((j + 1) * rows, rows)
            down = down + mm(left[:nrhs], low)
            if j:
                across = across + mm_nt(fields[j][:nrhs], low[: j * rows])
        total[j] = total[j] + down
        for i in range(j):
            total[i] = total[i] + across[:, i * rows : (i + 1) * rows]
        at += j + 1


def near_kernel(near, shape, *refs):
    high_ref, image_ref, low_ref = refs[near:]
    messages = [Message(shape, ref) for ref in refs[:near]]
    image = [jnp.zeros(image_ref.shape[1:], F32) for _ in range(near)]
    kern_columns(range(near), messages, high_ref, low_ref)
    add_products(range(near), high_ref, low_ref, [m.field() for m in messages], image)
    for s in range(near):
        image_ref[s] = image[s]


def far_kernel(slots, shape, near_image_ref, *refs):
    high_ref, image_ref, low_ref = refs[slots:]
    near = near_image_ref.shape[0]
    messages = [Message(shape, ref) for ref in refs[:slots]]
    image = [near_image_ref[s] for s in range(near)]
    image += [jnp.zeros(image_ref.shape[1:], F32) for _ in range(near, slots)]
    kern_columns(range(near, slots), messages, high_ref, low_ref)
    add_products(range(near, slots), high_ref, low_ref, [m.field() for m in messages], image)
    for s in range(slots):
        image_ref[s] = image[s]


def main_kernel(slots, shape, is_host_ref, near_high_ref, far_high_ref, image_ref, *refs):
    messages = [Message(shape, ref) for ref in refs[:slots]]
    proj_refs = refs[slots : 2 * slots]
    results = refs[2 * slots :]
    rows, _, levels, rank, nrhs = shape
    near = len(proj_refs) - 1
    mine = is_host_ref[0] == 1

    def put(s, at, value):
        value = jnp.where(mine, value, jnp.zeros_like(value)) if s == 0 else value
        results[s][at * nrhs : (at + 1) * nrhs] = value

    def put_halves(s, at, value):
        high = value.astype(BF16)
        low = (value - high.astype(F32)).astype(BF16)
        for k in range(rows // rank):
            put(s, at + 2 * k, high[:, k * rank : (k + 1) * rank])
            put(s, at + 2 * k + 1, low[:, k * rank : (k + 1) * rank])

    proj = []
    for level in range(levels):
        total = proj_refs[0][level * nrhs : (level + 1) * nrhs]
        for ref in proj_refs[1:]:
            total = total + ref[level * nrhs : (level + 1) * nrhs]
        proj.append(total.astype(BF16))
    fields = [message.field() for message in messages]
    field, image, image_b = [], [], []
    for s in range(slots):
        halves = fields[s].astype(F32)
        field.append(halves[:nrhs] + halves[nrhs:])
        total = image_ref[s] + 0.5 * field[s]
        for level in range(levels):
            total = total + mm_nt(proj[level], messages[s].factor(level))
        image.append(total)
        image_b.append(total.astype(BF16))
        put_halves(s, levels + 1, total)
    total = messages[0].project(image_b[0])
    for s in range(1, slots):
        total = total + messages[s].project(image_b[s])
    leaf_norm = jnp.sum(total[:nrhs] * total[:nrhs], axis=1, keepdims=True)
    for level in range(levels):
        part = total[level * nrhs : (level + 1) * nrhs].astype(BF16)
        for s in range(slots):
            put(s, level, part)
    second = [jnp.zeros((nrhs, rows), F32) for _ in range(slots)]
    add_products(range(near), near_high_ref, None, image_b, second)
    add_products(range(near, slots), far_high_ref, None, image_b, second)
    for s in range(slots):
        put_halves(s, levels + 1 + 2 * (rows // rank), second[s])

    def dots(left, right):
        total = left[0] * right[0]
        for s in range(1, slots):
            total = total + left[s] * right[s]
        return jnp.sum(total, axis=1, keepdims=True)

    scalars = [
        dots(field, field),
        dots(field, image),
        dots(image, image),
        dots(image, second) + leaf_norm,
    ]
    lane = lax.broadcasted_iota(jnp.int32, (nrhs, rank), 1)
    packed = jnp.zeros((nrhs, rank), F32)
    for k, value in enumerate(scalars):
        value = jnp.broadcast_to(value, (nrhs, rank))
        for piece in range(3):
            rounded = value.astype(BF16).astype(F32)
            packed = jnp.where(lane == 3 * k + piece, rounded, packed)
            value = value - rounded
    for s in range(slots):
        put(s, levels, packed.astype(BF16))


def finish_kernel(leaves, field_ref, factors_ref, result_ref, *refs):
    sums = refs[:leaves]
    solution_ref, residual_ref = refs[leaves:]
    levels, rows, rank = factors_ref.shape
    nrhs = field_ref.shape[0]
    field = field_ref[...]

    def halves(at):
        pieces = []
        for k in range(rows // rank):
            start = (at + 2 * k) * nrhs
            piece = result_ref[start : start + 2 * nrhs].astype(F32)
            pieces.append(piece[:nrhs] + piece[nrhs:])
        return jnp.concatenate(pieces, axis=1)

    image = halves(levels + 1)
    second = halves(levels + 1 + 2 * (rows // rank)) + 0.5 * image
    lane = lax.broadcasted_iota(jnp.int32, (nrhs, rank), 1)
    packed = sums[0][levels * nrhs :].astype(F32)
    for m in range(1, leaves):
        packed = packed + sums[m][levels * nrhs :].astype(F32)

    def scalar(k):
        inside = (lane >= 3 * k) & (lane < 3 * k + 3)
        return jnp.sum(jnp.where(inside, packed, 0.0), axis=1, keepdims=True)

    bb, bw, ww, wu = (scalar(k) for k in range(4))
    wu = wu + 0.5 * ww
    for level in range(levels):
        nodes = {}
        for m in range(leaves):
            value = sums[m][level * nrhs : (level + 1) * nrhs].astype(F32)
            node = m >> level
            nodes[node] = nodes[node] + value if node in nodes else value
        second = second + mm_nt(nodes[0].astype(BF16), factors_ref[level])
        if level > 0:
            squared = sum(value * value for value in nodes.values())
            wu = wu + jnp.sum(squared, axis=1, keepdims=True)
    alpha0 = bb / bw
    norm1 = alpha0 * alpha0 * ww - bb
    ratio = norm1 / bb
    keep = 1.0 + ratio
    curv = keep * keep * bw - 2.0 * keep * alpha0 * ww + alpha0 * alpha0 * wu
    alpha1 = norm1 / curv
    solution_ref[...] = (alpha0 + alpha1 * keep) * field - (alpha1 * alpha0) * image
    residual_ref[...] = field - (alpha0 + alpha1 * keep) * image + (alpha1 * alpha0) * second


def call(kernel, outs, args, specs, scratch=(), flops=0, limit=24):
    moved = sum(a.size * a.dtype.itemsize for a in args)
    return pl.pallas_call(
        kernel,
        out_shape=[jax.ShapeDtypeStruct(shape, dtype) for shape, dtype in outs],
        in_specs=specs,
        out_specs=[VMEM] * len(outs),
        scratch_shapes=list(scratch),
        cost_estimate=pl.CostEstimate(flops=flops, bytes_accessed=moved, transcendentals=0),
        compiler_params=pltpu.CompilerParams(vmem_limit_bytes=limit * 2**20),
    )(*args)


def collected(embed, factors, targets):
    leaves, inner = lax.axis_size("leaf"), lax.axis_size("inner")
    levels, rows, rank = factors.shape
    nrhs = targets.shape[1]
    dims = embed.shape[1]
    shape = (rows, dims, levels, rank, nrhs)

    def host(leaf):
        return inner // 2 if leaf % 2 == 0 else (inner - 1) // 2

    def others(leaf):
        sign = 1 if leaf % 2 == 0 else -1
        here = host(leaf)
        return sorted((z for z in range(inner) if z != here), key=lambda z: (abs(z - here), sign * z))

    routes = [
        [(leaf * inner + others(leaf)[k], leaf * inner + host(leaf)) for leaf in range(leaves)]
        for k in range(inner - 1)
    ]

    axes = ("leaf", "inner")

    def from_host(values):
        back = [
            lax.ppermute(value, axes, [(b, a) for a, b in route])
            for value, route in zip(values[1:], routes)
        ]
        return [values[0]] + back

    def to_host(value):
        return [value] + [lax.ppermute(value, axes, route) for route in routes]

    def over_leaf(value, m):
        return lax.ppermute(value, "leaf", [(i, i ^ m) for i in range(leaves)])

    field = targets.T
    height = dims // rank * rows + 2 * nrhs * (rows // rank) + levels * rows
    hbm = pl.BlockSpec(memory_space=pltpu.HBM)
    (message,) = call(
        pack_kernel,
        [((height, rank), BF16)],
        [embed, factors, field],
        [hbm] * 3,
        scratch=[
            pltpu.VMEM((nrhs, rows), F32),
            pltpu.SemaphoreType.DMA((1 + dims // rank + levels,)),
        ],
        limit=60,
    )
    messages = to_host(message)
    first, upper = call(
        project_kernel,
        [((nrhs, rank), F32), (((levels - 1) * nrhs, rank), F32)],
        [factors, field],
        [VMEM] * 2,
    )
    projs = [first]
    for bit in range(levels - 1):
        upper = upper + over_leaf(upper, 2**bit)
        projs.append(upper[:nrhs])
        upper = upper[nrhs:]
    projs = to_host(jnp.concatenate(projs, axis=0))
    near = inner - 1
    held, pairs = len(pairs_of(near)), len(pairs_of(inner))
    near_high, near_image = call(
        functools.partial(near_kernel, near, shape),
        [((held, rows, rows), BF16), ((near, nrhs, rows), F32)],
        messages[:near],
        [VMEM] * near,
        scratch=[pltpu.VMEM((held, rows, rows), BF16)],
        flops=NEAR_FLOPS,
    )
    far_high, image = call(
        functools.partial(far_kernel, inner, shape),
        [((pairs - held, rows, rows), BF16), ((inner, nrhs, rows), F32)],
        [near_image] + messages,
        [VMEM] * (1 + inner),
        scratch=[pltpu.VMEM((pairs - held, rows, rows), BF16)],
        flops=FAR_FLOPS,
    )
    leaf = lax.axis_index("leaf")
    here = jnp.where(leaf % 2 == 0, host(0), host(1))
    is_host = (lax.axis_index("inner") == here).astype(jnp.int32).reshape(1)
    height = (levels + 1 + 4 * (rows // rank)) * nrhs
    results = call(
        functools.partial(main_kernel, inner, shape),
        [((height, rank), BF16)] * inner,
        [is_host, near_high, far_high, image] + messages + projs,
        [SMEM] + [VMEM] * (3 + 2 * inner),
        flops=MAIN_FLOPS,
    )
    result = results[0]
    for value, route in reversed(list(zip(results[1:], routes))):
        result = result + lax.ppermute(value, axes, [(b, a) for a, b in route])
    sums = result[: (levels + 1) * nrhs]
    leaf_sums = [sums] + [over_leaf(sums, m) for m in range(1, leaves)]
    answer, residual = call(
        functools.partial(finish_kernel, leaves),
        [((nrhs, rows), F32)] * 2,
        [field, factors, result] + leaf_sums,
        [VMEM] * (3 + leaves),
    )
    return (answer.T, residual.T)


def on_device(embed, factors, targets):
    if embed.shape[0] * lax.axis_size("inner") <= FAST_LEAF:
        return collected(embed, factors, targets)
    return stepwise(embed, factors, targets)


def solution(mesh):
    return jax.shard_map(
        on_device,
        mesh=mesh,
        in_specs=(
            P(("groups", "leaf", "inner"), None),
            P(None, ("groups", "leaf", "inner"), None),
            P(("groups", "leaf", "inner"), None),
        ),
        out_specs=(P(("groups", "leaf", "inner"), None), P(("groups", "leaf", "inner"), None)),
        check_vma=False,
    )
```

```python
import functools

import jax
import jax.numpy as jnp
from jax import lax
from jax.experimental import pallas as pl
from jax.experimental.pallas import tpu as pltpu
from jax.sharding import PartitionSpec as P

ITERS = 2
LENGTH_SCALE = 2.3
FAST_LEAF = 2048
NEAR_FLOPS = 4 * 10**9
FAR_FLOPS = 3 * 10**9
MAIN_FLOPS = 2 * 10**9
F32, BF16 = jnp.float32, jnp.bfloat16
VMEM = pl.BlockSpec(memory_space=pltpu.VMEM)
SMEM = pl.BlockSpec(memory_space=pltpu.SMEM)


def swapped(value, axis, apart):
    mask = 2**apart
    pairs = [(source, source ^ mask) for source in range(lax.axis_size(axis))]
    return lax.ppermute(value, axis, pairs)


def matern(left, right):
    left_f = left.astype(F32)
    right_f = right.astype(F32)
    left_sq = jnp.sum(left_f * left_f, axis=1)
    right_sq = jnp.sum(right_f * right_f, axis=1)
    inner_prod = lax.dot_general(
        left, right, (((1,), (1,)), ((), ())), preferred_element_type=F32
    )
    dist2 = left_sq[:, None] + right_sq[None, :] - 2.0 * inner_prod
    scaled = jnp.sqrt(3.0) * jnp.sqrt(jnp.maximum(dist2, 0.0)) / LENGTH_SCALE
    return (1.0 + scaled) * jnp.exp(-scaled)


def squares(residual):
    return lax.psum(jnp.sum(residual * residual, axis=0), ("leaf", "inner"))


def operate(embed, factors, field):
    piece = lax.all_gather(embed, "inner", axis=0, tiled=True)
    terms = jnp.dot(matern(piece, embed), field, precision=lax.Precision.HIGHEST)
    dense = lax.psum_scatter(terms, "inner", scatter_dimension=0, tiled=True)
    total = dense + 0.5 * field
    levels = factors.shape[0]
    rounded = field.astype(BF16)
    proj = jnp.einsum("lrk,rc->lkc", factors, rounded, preferred_element_type=F32)
    proj = lax.psum(proj, "inner")
    for bit in range(levels - 1):
        upper = proj[bit + 1 :]
        partner = swapped(upper, "leaf", bit)
        proj = jnp.concatenate([proj[: bit + 1], upper + partner], axis=0)
    back = jnp.einsum(
        "lrk,lkc->rc", factors, proj.astype(BF16), preferred_element_type=F32
    )
    return total + back


def stepwise(embed, factors, targets):
    result = jnp.zeros_like(targets)
    residual = targets
    direction = targets
    norm_now = squares(residual)
    for step in range(ITERS):
        image = operate(embed, factors, direction)
        curv = lax.psum(jnp.sum(direction * image, axis=0), ("leaf", "inner"))
        alpha = norm_now / curv
        result = result + alpha * direction
        residual = residual - alpha * image
        if step + 1 < ITERS:
            norm_next = squares(residual)
            direction = residual + norm_next / norm_now * direction
            norm_now = norm_next
    return (result, residual)


def mm(left, right):
    return lax.dot_general(left, right, (((1,), (0,)), ((), ())), preferred_element_type=F32)


def mm_nt(left, right):
    return lax.dot_general(left, right, (((1,), (1,)), ((), ())), preferred_element_type=F32)


def pairs_of(slots):
    return [(i, j) for j in range(slots) for i in range(j + 1)]


def put_halves(ref, start, value):
    rows = value.shape[0]
    high = value.astype(BF16)
    ref[start : start + rows] = high
    ref[start + rows : start + 2 * rows] = (value - high.astype(F32)).astype(BF16)


def pack_kernel(embed_ref, factors_ref, field_ref, head_ref, tail_ref, first_ref, upper_ref):
    levels, rows, rank = factors_ref.shape
    nrhs = field_ref.shape[0]
    lanes = embed_ref.shape[1] // rank
    rounded = field_ref[...].astype(BF16)
    first_ref[...] = mm(rounded, factors_ref[0])
    for level in range(1, levels):
        upper_ref[(level - 1) * nrhs : level * nrhs] = mm(rounded, factors_ref[level])
    for k in range(lanes):
        head_ref[k * rows : (k + 1) * rows] = embed_ref[:, k * rank : (k + 1) * rank]
    for k in range(rows // rank):
        put_halves(head_ref, lanes * rows + 2 * k * nrhs, field_ref[:, k * rank : (k + 1) * rank])
    for level in range(levels):
        tail_ref[level * rows : (level + 1) * rows] = factors_ref[level]


def tail_kernel(start, tail_in, *refs):
    del tail_in
    *proj_refs, tail_ref = refs
    for ref in proj_refs:
        put_halves(tail_ref, start, ref[...])
        start += 2 * ref.shape[0]


class Message:
    def __init__(self, shape, head_ref=None, tail_ref=None):
        self.rows, self.dims, self.levels, self.rank, self.nrhs = shape
        self.head = head_ref
        self.tail = tail_ref

    def embed(self):
        rows = self.rows
        pieces = [self.head[k * rows : (k + 1) * rows] for k in range(self.dims // self.rank)]
        return jnp.concatenate(pieces, axis=1)

    def field(self):
        base = self.dims // self.rank * self.rows
        step = 2 * self.nrhs
        count = self.rows // self.rank
        pieces = [self.head[base + k * step : base + (k + 1) * step] for k in range(count)]
        return jnp.concatenate(pieces, axis=1)

    def factor(self, level):
        return self.tail[level * self.rows : (level + 1) * self.rows]

    def proj(self, level):
        base = self.levels * self.rows + 2 * level * self.nrhs
        halves = self.tail[base : base + 2 * self.nrhs].astype(F32)
        return halves[: self.nrhs] + halves[self.nrhs :]

    def project(self, field):
        return jnp.concatenate([mm(field, self.factor(l)) for l in range(self.levels)], axis=0)


def norms_of(embed):
    scale = 3.0 / LENGTH_SCALE**2
    wide_e = embed.astype(F32)
    square = wide_e * wide_e
    column = scale * jnp.sum(square, axis=1, keepdims=True)
    first = square.astype(BF16)
    rest = (square - first.astype(F32)).astype(BF16)
    ones = jnp.ones((8, embed.shape[1]), BF16)
    row = scale * (mm_nt(ones, first) + mm_nt(ones, rest))
    return column, row[0:1]


def kern_block(left, right, column, row):
    scale = 3.0 / LENGTH_SCALE**2
    product = mm_nt(left, right)
    dist = jnp.maximum((column + row) - (2.0 * scale) * product, 1e-30)
    scaled = dist * lax.rsqrt(dist)
    value = (1.0 + scaled) * jnp.exp(-scaled)
    high = value.astype(BF16)
    return high, (value - high.astype(F32)).astype(BF16)


def kern_columns(columns, messages, high_ref, low_ref):
    norms = {}
    index = 0
    for j in columns:
        for i in range(j + 1):
            for s in (i, j):
                if s not in norms:
                    norms[s] = norms_of(messages[s].embed())
            high_ref[index], low_ref[index] = kern_block(
                messages[i].embed(), messages[j].embed(), norms[i][0], norms[j][1]
            )
            index += 1


def add_products(columns, high_ref, low_ref, fields, total):
    nrhs, rows = total[0].shape

    def fold(stacked):
        return stacked[:nrhs] + stacked[nrhs:] if stacked.shape[0] > nrhs else stacked

    at = 0
    for j in columns:
        left = jnp.concatenate(fields[: j + 1], axis=1)
        high = high_ref[at : at + j + 1].reshape((j + 1) * rows, rows)
        down = fold(mm(left, high))
        across = fold(mm_nt(fields[j], high[: j * rows])) if j else None
        if low_ref is not None:
            low = low_ref[at : at + j + 1].reshape((j + 1) * rows, rows)
            down = down + mm(left[:nrhs], low)
            if j:
                across = across + mm_nt(fields[j][:nrhs], low[: j * rows])
        total[j] = total[j] + down
        for i in range(j):
            total[i] = total[i] + across[:, i * rows : (i + 1) * rows]
        at += j + 1


def near_kernel(near, shape, *refs):
    high_ref, image_ref, low_ref = refs[near:]
    messages = [Message(shape, ref) for ref in refs[:near]]
    image = [jnp.zeros(image_ref.shape[1:], F32) for _ in range(near)]
    kern_columns(range(near), messages, high_ref, low_ref)
    add_products(range(near), high_ref, low_ref, [m.field() for m in messages], image)
    for s in range(near):
        image_ref[s] = image[s]


def far_kernel(slots, shape, near_image_ref, *refs):
    high_ref, image_ref, low_ref = refs[slots:]
    near = near_image_ref.shape[0]
    messages = [Message(shape, ref) for ref in refs[:slots]]
    image = [near_image_ref[s] for s in range(near)]
    image += [jnp.zeros(image_ref.shape[1:], F32) for _ in range(near, slots)]
    kern_columns(range(near, slots), messages, high_ref, low_ref)
    add_products(range(near, slots), high_ref, low_ref, [m.field() for m in messages], image)
    for s in range(slots):
        image_ref[s] = image[s]


def main_kernel(slots, shape, is_host_ref, near_high_ref, far_high_ref, image_ref, *refs):
    messages = [Message(shape, refs[s], refs[slots + s]) for s in range(slots)]
    results = refs[2 * slots :]
    rows, _, levels, rank, nrhs = shape
    near = slots - 1
    mine = is_host_ref[0] == 1

    def put(s, at, value):
        value = jnp.where(mine, value, jnp.zeros_like(value)) if s == 0 else value
        results[s][at * nrhs : (at + 1) * nrhs] = value

    def put_halves(s, at, value):
        high = value.astype(BF16)
        low = (value - high.astype(F32)).astype(BF16)
        for k in range(rows // rank):
            put(s, at + 2 * k, high[:, k * rank : (k + 1) * rank])
            put(s, at + 2 * k + 1, low[:, k * rank : (k + 1) * rank])

    proj = []
    for level in range(levels):
        total = messages[0].proj(level)
        for message in messages[1:]:
            total = total + message.proj(level)
        proj.append(total.astype(BF16))
    fields = [message.field() for message in messages]
    field, image, image_b = [], [], []
    for s in range(slots):
        halves = fields[s].astype(F32)
        field.append(halves[:nrhs] + halves[nrhs:])
        total = image_ref[s] + 0.5 * field[s]
        for level in range(levels):
            total = total + mm_nt(proj[level], messages[s].factor(level))
        image.append(total)
        image_b.append(total.astype(BF16))
        put_halves(s, levels + 1, total)
    total = messages[0].project(image_b[0])
    for s in range(1, slots):
        total = total + messages[s].project(image_b[s])
    leaf_norm = jnp.sum(total[:nrhs] * total[:nrhs], axis=1, keepdims=True)
    for level in range(levels):
        part = total[level * nrhs : (level + 1) * nrhs].astype(BF16)
        for s in range(slots):
            put(s, level, part)
    second = [jnp.zeros((nrhs, rows), F32) for _ in range(slots)]
    add_products(range(near), near_high_ref, None, image_b, second)
    add_products(range(near, slots), far_high_ref, None, image_b, second)
    for s in range(slots):
        put_halves(s, levels + 1 + 2 * (rows // rank), second[s])

    def dots(left, right):
        total = left[0] * right[0]
        for s in range(1, slots):
            total = total + left[s] * right[s]
        return jnp.sum(total, axis=1, keepdims=True)

    scalars = [
        dots(field, field),
        dots(field, image),
        dots(image, image),
        dots(image, second) + leaf_norm,
    ]
    lane = lax.broadcasted_iota(jnp.int32, (nrhs, rank), 1)
    packed = jnp.zeros((nrhs, rank), F32)
    for k, value in enumerate(scalars):
        value = jnp.broadcast_to(value, (nrhs, rank))
        for piece in range(3):
            rounded = value.astype(BF16).astype(F32)
            packed = jnp.where(lane == 3 * k + piece, rounded, packed)
            value = value - rounded
    for s in range(slots):
        put(s, levels, packed.astype(BF16))


def finish_kernel(leaves, field_ref, factors_ref, result_ref, *refs):
    sums = refs[:leaves]
    solution_ref, residual_ref = refs[leaves:]
    levels, rows, rank = factors_ref.shape
    nrhs = field_ref.shape[0]
    field = field_ref[...]

    def halves(at):
        pieces = []
        for k in range(rows // rank):
            start = (at + 2 * k) * nrhs
            piece = result_ref[start : start + 2 * nrhs].astype(F32)
            pieces.append(piece[:nrhs] + piece[nrhs:])
        return jnp.concatenate(pieces, axis=1)

    image = halves(levels + 1)
    second = halves(levels + 1 + 2 * (rows // rank)) + 0.5 * image
    lane = lax.broadcasted_iota(jnp.int32, (nrhs, rank), 1)
    packed = sums[0][levels * nrhs :].astype(F32)
    for m in range(1, leaves):
        packed = packed + sums[m][levels * nrhs :].astype(F32)

    def scalar(k):
        inside = (lane >= 3 * k) & (lane < 3 * k + 3)
        return jnp.sum(jnp.where(inside, packed, 0.0), axis=1, keepdims=True)

    bb, bw, ww, wu = (scalar(k) for k in range(4))
    wu = wu + 0.5 * ww
    for level in range(levels):
        nodes = {}
        for m in range(leaves):
            value = sums[m][level * nrhs : (level + 1) * nrhs].astype(F32)
            node = m >> level
            nodes[node] = nodes[node] + value if node in nodes else value
        second = second + mm_nt(nodes[0].astype(BF16), factors_ref[level])
        if level > 0:
            squared = sum(value * value for value in nodes.values())
            wu = wu + jnp.sum(squared, axis=1, keepdims=True)
    alpha0 = bb / bw
    norm1 = alpha0 * alpha0 * ww - bb
    ratio = norm1 / bb
    keep = 1.0 + ratio
    curv = keep * keep * bw - 2.0 * keep * alpha0 * ww + alpha0 * alpha0 * wu
    alpha1 = norm1 / curv
    solution_ref[...] = (alpha0 + alpha1 * keep) * field - (alpha1 * alpha0) * image
    residual_ref[...] = field - (alpha0 + alpha1 * keep) * image + (alpha1 * alpha0) * second


def call(kernel, outs, args, specs, scratch=(), flops=0, limit=24, aliases={}):
    moved = sum(a.size * a.dtype.itemsize for a in args)
    return pl.pallas_call(
        kernel,
        out_shape=[jax.ShapeDtypeStruct(shape, dtype) for shape, dtype in outs],
        in_specs=specs,
        out_specs=[VMEM] * len(outs),
        scratch_shapes=list(scratch),
        input_output_aliases=aliases,
        cost_estimate=pl.CostEstimate(flops=flops, bytes_accessed=moved, transcendentals=0),
        compiler_params=pltpu.CompilerParams(vmem_limit_bytes=limit * 2**20),
    )(*args)


def collected(embed, factors, targets):
    leaves, inner = lax.axis_size("leaf"), lax.axis_size("inner")
    levels, rows, rank = factors.shape
    dims, nrhs = embed.shape[1], targets.shape[1]
    shape = (rows, dims, levels, rank, nrhs)

    def host(leaf):
        return inner // 2 if leaf % 2 == 0 else (inner - 1) // 2

    def others(leaf):
        sign = 1 if leaf % 2 == 0 else -1
        here = host(leaf)
        return sorted((z for z in range(inner) if z != here), key=lambda z: (abs(z - here), sign * z))

    routes = [
        [(leaf * inner + others(leaf)[k], leaf * inner + host(leaf)) for leaf in range(leaves)]
        for k in range(inner - 1)
    ]

    axes = ("leaf", "inner")

    def from_host(values):
        back = [
            lax.ppermute(value, axes, [(b, a) for a, b in route])
            for value, route in zip(values[1:], routes)
        ]
        return [values[0]] + back

    def to_host(value):
        return [value] + [lax.ppermute(value, axes, route) for route in routes]

    def over_leaf(value, m):
        return lax.ppermute(value, "leaf", [(i, i ^ m) for i in range(leaves)])

    field = targets.T
    near = inner - 1
    held, pairs = len(pairs_of(near)), len(pairs_of(inner))
    head = dims // rank * rows + 2 * nrhs * (rows // rank)
    tail = levels * (rows + 2 * nrhs)
    sizes = [((head, rank), BF16), ((tail, rank), BF16)]
    sizes += [((nrhs, rank), F32), (((levels - 1) * nrhs, rank), F32)]
    first_part, second_part, first, upper = call(
        pack_kernel, sizes, [embed, factors, targets.T], [VMEM] * 3
    )
    heads = to_host(first_part)
    proj = [first]
    for bit in range(levels - 1):
        upper = upper + over_leaf(upper, 2**bit)
        proj.append(upper[:nrhs])
        upper = upper[nrhs:]
    (second_part,) = call(
        functools.partial(tail_kernel, levels * rows),
        [sizes[1]],
        [second_part] + proj,
        [VMEM] * (1 + levels),
        aliases={0: 0},
    )
    tails = to_host(second_part)
    near_high, near_image = call(
        functools.partial(near_kernel, near, shape),
        [((held, rows, rows), BF16), ((near, nrhs, rows), F32)],
        heads[:near],
        [VMEM] * near,
        scratch=[pltpu.VMEM((held, rows, rows), BF16)],
        flops=NEAR_FLOPS,
    )
    far_high, image = call(
        functools.partial(far_kernel, inner, shape),
        [((pairs - held, rows, rows), BF16), ((inner, nrhs, rows), F32)],
        [near_image] + heads,
        [VMEM] * (1 + inner),
        scratch=[pltpu.VMEM((pairs - held, rows, rows), BF16)],
        flops=FAR_FLOPS,
    )
    leaf = lax.axis_index("leaf")
    here = jnp.where(leaf % 2 == 0, host(0), host(1))
    is_host = (lax.axis_index("inner") == here).astype(jnp.int32).reshape(1)
    height = (levels + 1 + 4 * (rows // rank)) * nrhs
    results = call(
        functools.partial(main_kernel, inner, shape),
        [((height, rank), BF16)] * inner,
        [is_host, near_high, far_high, image] + heads + tails,
        [SMEM] + [VMEM] * (3 + 2 * inner),
        flops=MAIN_FLOPS,
    )
    result = results[0]
    for value, route in reversed(list(zip(results[1:], routes))):
        result = result + lax.ppermute(value, axes, [(b, a) for a, b in route])
    sums = result[: (levels + 1) * nrhs]
    leaf_sums = [sums] + [over_leaf(sums, m) for m in range(1, leaves)]
    answer, residual = call(
        functools.partial(finish_kernel, leaves),
        [((nrhs, rows), F32)] * 2,
        [field, factors, result] + leaf_sums,
        [VMEM] * (3 + leaves),
    )
    return (answer.T, residual.T)


def on_device(embed, factors, targets):
    if embed.shape[0] * lax.axis_size("inner") <= FAST_LEAF:
        return collected(embed, factors, targets)
    return stepwise(embed, factors, targets)


def solution(mesh):
    return jax.shard_map(
        on_device,
        mesh=mesh,
        in_specs=(
            P(("groups", "leaf", "inner"), None),
            P(None, ("groups", "leaf", "inner"), None),
            P(("groups", "leaf", "inner"), None),
        ),
        out_specs=(P(("groups", "leaf", "inner"), None), P(("groups", "leaf", "inner"), None)),
        check_vma=False,
    )
```

```python
import functools

import jax
import jax.numpy as jnp
from jax import lax
from jax.experimental import pallas as pl
from jax.experimental.pallas import tpu as pltpu
from jax.sharding import PartitionSpec as P

ITERS = 2
LENGTH_SCALE = 2.3
FAST_LEAF = 2048
NEAR_FLOPS = 4 * 10**9
FAR_FLOPS = 3 * 10**9
MAIN_FLOPS = 2 * 10**9
F32, BF16 = jnp.float32, jnp.bfloat16
VMEM = pl.BlockSpec(memory_space=pltpu.VMEM)
SMEM = pl.BlockSpec(memory_space=pltpu.SMEM)


def swapped(value, axis, apart):
    mask = 2**apart
    pairs = [(source, source ^ mask) for source in range(lax.axis_size(axis))]
    return lax.ppermute(value, axis, pairs)


def matern(left, right):
    left_f = left.astype(F32)
    right_f = right.astype(F32)
    left_sq = jnp.sum(left_f * left_f, axis=1)
    right_sq = jnp.sum(right_f * right_f, axis=1)
    inner_prod = lax.dot_general(
        left, right, (((1,), (1,)), ((), ())), preferred_element_type=F32
    )
    dist2 = left_sq[:, None] + right_sq[None, :] - 2.0 * inner_prod
    scaled = jnp.sqrt(3.0) * jnp.sqrt(jnp.maximum(dist2, 0.0)) / LENGTH_SCALE
    return (1.0 + scaled) * jnp.exp(-scaled)


def squares(residual):
    return lax.psum(jnp.sum(residual * residual, axis=0), ("leaf", "inner"))


def operate(embed, factors, field):
    piece = lax.all_gather(embed, "inner", axis=0, tiled=True)
    terms = jnp.dot(matern(piece, embed), field, precision=lax.Precision.HIGHEST)
    dense = lax.psum_scatter(terms, "inner", scatter_dimension=0, tiled=True)
    total = dense + 0.5 * field
    levels = factors.shape[0]
    rounded = field.astype(BF16)
    proj = jnp.einsum("lrk,rc->lkc", factors, rounded, preferred_element_type=F32)
    proj = lax.psum(proj, "inner")
    for bit in range(levels - 1):
        upper = proj[bit + 1 :]
        partner = swapped(upper, "leaf", bit)
        proj = jnp.concatenate([proj[: bit + 1], upper + partner], axis=0)
    back = jnp.einsum(
        "lrk,lkc->rc", factors, proj.astype(BF16), preferred_element_type=F32
    )
    return total + back


def stepwise(embed, factors, targets):
    result = jnp.zeros_like(targets)
    residual = targets
    direction = targets
    norm_now = squares(residual)
    for step in range(ITERS):
        image = operate(embed, factors, direction)
        curv = lax.psum(jnp.sum(direction * image, axis=0), ("leaf", "inner"))
        alpha = norm_now / curv
        result = result + alpha * direction
        residual = residual - alpha * image
        if step + 1 < ITERS:
            norm_next = squares(residual)
            direction = residual + norm_next / norm_now * direction
            norm_now = norm_next
    return (result, residual)


def mm(left, right):
    return lax.dot_general(left, right, (((1,), (0,)), ((), ())), preferred_element_type=F32)


def mm_nt(left, right):
    return lax.dot_general(left, right, (((1,), (1,)), ((), ())), preferred_element_type=F32)


def pairs_of(slots):
    return [(i, j) for j in range(slots) for i in range(j + 1)]


def put_halves(ref, start, value):
    rows = value.shape[0]
    high = value.astype(BF16)
    ref[start : start + rows] = high
    ref[start + rows : start + 2 * rows] = (value - high.astype(F32)).astype(BF16)


def pack_kernel(embed_ref, factors_ref, field_ref, head_ref, tail_ref, first_ref, upper_ref):
    levels, rows, rank = factors_ref.shape
    nrhs = field_ref.shape[0]
    lanes = embed_ref.shape[1] // rank
    rounded = field_ref[...].astype(BF16)
    first_ref[...] = mm(rounded, factors_ref[0])
    for level in range(1, levels):
        upper_ref[(level - 1) * nrhs : level * nrhs] = mm(rounded, factors_ref[level])
    for k in range(lanes):
        head_ref[k * rows : (k + 1) * rows] = embed_ref[:, k * rank : (k + 1) * rank]
    for k in range(rows // rank):
        put_halves(head_ref, lanes * rows + 2 * k * nrhs, field_ref[:, k * rank : (k + 1) * rank])
    for level in range(levels):
        tail_ref[level * rows : (level + 1) * rows] = factors_ref[level]


def tail_kernel(start, tail_in, *refs):
    del tail_in
    *proj_refs, tail_ref = refs
    for ref in proj_refs:
        put_halves(tail_ref, start, ref[...])
        start += 2 * ref.shape[0]


class Message:
    def __init__(self, shape, head_ref=None, tail_ref=None):
        self.rows, self.dims, self.levels, self.rank, self.nrhs = shape
        self.head = head_ref
        self.tail = tail_ref

    def embed(self):
        rows = self.rows
        pieces = [self.head[k * rows : (k + 1) * rows] for k in range(self.dims // self.rank)]
        return jnp.concatenate(pieces, axis=1)

    def field(self):
        base = self.dims // self.rank * self.rows
        step = 2 * self.nrhs
        count = self.rows // self.rank
        pieces = [self.head[base + k * step : base + (k + 1) * step] for k in range(count)]
        return jnp.concatenate(pieces, axis=1)

    def factor(self, level):
        return self.tail[level * self.rows : (level + 1) * self.rows]

    def proj(self, level):
        base = self.levels * self.rows + 2 * level * self.nrhs
        halves = self.tail[base : base + 2 * self.nrhs].astype(F32)
        return halves[: self.nrhs] + halves[self.nrhs :]

    def project(self, field):
        return jnp.concatenate([mm(field, self.factor(l)) for l in range(self.levels)], axis=0)


def norms_of(embed):
    scale = 3.0 / LENGTH_SCALE**2
    wide_e = embed.astype(F32)
    square = wide_e * wide_e
    column = scale * jnp.sum(square, axis=1, keepdims=True)
    first = square.astype(BF16)
    rest = (square - first.astype(F32)).astype(BF16)
    ones = jnp.ones((8, embed.shape[1]), BF16)
    row = scale * (mm_nt(ones, first) + mm_nt(ones, rest))
    return column, row[0:1]


def kern_block(left, right, column, row):
    scale = 3.0 / LENGTH_SCALE**2
    product = mm_nt(left, right)
    dist = jnp.maximum((column + row) - (2.0 * scale) * product, 1e-30)
    scaled = dist * lax.rsqrt(dist)
    value = (1.0 + scaled) * jnp.exp(-scaled)
    high = value.astype(BF16)
    return high, (value - high.astype(F32)).astype(BF16)


def kern_columns(columns, messages, high_ref, low_ref):
    norms = {}
    index = 0
    for j in columns:
        for i in range(j + 1):
            for s in (i, j):
                if s not in norms:
                    norms[s] = norms_of(messages[s].embed())
            high_ref[index], low_ref[index] = kern_block(
                messages[i].embed(), messages[j].embed(), norms[i][0], norms[j][1]
            )
            index += 1


def add_products(columns, high_ref, low_ref, fields, total):
    nrhs, rows = total[0].shape

    def fold(stacked):
        return stacked[:nrhs] + stacked[nrhs:] if stacked.shape[0] > nrhs else stacked

    at = 0
    for j in columns:
        left = jnp.concatenate(fields[: j + 1], axis=1)
        high = high_ref[at : at + j + 1].reshape((j + 1) * rows, rows)
        down = fold(mm(left, high))
        across = fold(mm_nt(fields[j], high[: j * rows])) if j else None
        if low_ref is not None:
            low = low_ref[at : at + j + 1].reshape((j + 1) * rows, rows)
            down = down + mm(left[:nrhs], low)
            if j:
                across = across + mm_nt(fields[j][:nrhs], low[: j * rows])
        total[j] = total[j] + down
        for i in range(j):
            total[i] = total[i] + across[:, i * rows : (i + 1) * rows]
        at += j + 1


def near_kernel(near, shape, is_host_ref, *refs):
    @pl.when(is_host_ref[0] == 1)
    def _():
        high_ref, image_ref, low_ref = refs[near:]
        messages = [Message(shape, ref) for ref in refs[:near]]
        image = [jnp.zeros(image_ref.shape[1:], F32) for _ in range(near)]
        kern_columns(range(near), messages, high_ref, low_ref)
        add_products(range(near), high_ref, low_ref, [m.field() for m in messages], image)
        for s in range(near):
            image_ref[s] = image[s]


def far_kernel(slots, shape, is_host_ref, near_image_ref, *refs):
    @pl.when(is_host_ref[0] == 1)
    def _():
        high_ref, image_ref, low_ref = refs[slots:]
        near = near_image_ref.shape[0]
        messages = [Message(shape, ref) for ref in refs[:slots]]
        image = [near_image_ref[s] for s in range(near)]
        image += [jnp.zeros(image_ref.shape[1:], F32) for _ in range(near, slots)]
        kern_columns(range(near, slots), messages, high_ref, low_ref)
        add_products(range(near, slots), high_ref, low_ref, [m.field() for m in messages], image)
        for s in range(slots):
            image_ref[s] = image[s]


def sending_order(slots):
    count = slots - 1
    return [1, 0] + list(range(2, count)) if count > 1 else list(range(count))


def tail_order(slots):
    sent = sorted(range(1, slots), key=lambda slot: sending_order(slots)[slot - 1])
    return [0] + sent[::-1]


def main_kernel(slots, shape, is_host_ref, near_high_ref, far_high_ref, image_ref, *refs):
    results = refs[2 * slots :]

    @pl.when(is_host_ref[0] == 0)
    def _():
        results[0][...] = jnp.zeros_like(results[0])

    @pl.when(is_host_ref[0] == 1)
    def _():
        order = tail_order(slots)
        messages = [Message(shape, refs[s], refs[slots + order.index(s)]) for s in range(slots)]
        rows, _, levels, rank, nrhs = shape
        near = slots - 1

        def put(s, at, value):
            results[s][at * nrhs : (at + 1) * nrhs] = value

        def put_halves(s, at, value):
            high = value.astype(BF16)
            low = (value - high.astype(F32)).astype(BF16)
            for k in range(rows // rank):
                put(s, at + 2 * k, high[:, k * rank : (k + 1) * rank])
                put(s, at + 2 * k + 1, low[:, k * rank : (k + 1) * rank])

        proj = []
        for level in range(levels):
            total = messages[0].proj(level)
            for message in messages[1:]:
                total = total + message.proj(level)
            proj.append(total.astype(BF16))
        fields = [message.field() for message in messages]
        field, image, image_b = [], [], []
        for s in range(slots):
            halves = fields[s].astype(F32)
            field.append(halves[:nrhs] + halves[nrhs:])
            total = image_ref[s] + 0.5 * field[s]
            for level in range(levels):
                total = total + mm_nt(proj[level], messages[s].factor(level))
            image.append(total)
            image_b.append(total.astype(BF16))
            put_halves(s, levels + 1, total)
        total = messages[0].project(image_b[0])
        for s in range(1, slots):
            total = total + messages[s].project(image_b[s])
        leaf_norm = jnp.sum(total[:nrhs] * total[:nrhs], axis=1, keepdims=True)
        for level in range(levels):
            part = total[level * nrhs : (level + 1) * nrhs].astype(BF16)
            for s in range(slots):
                put(s, level, part)
        second = [jnp.zeros((nrhs, rows), F32) for _ in range(slots)]
        add_products(range(near), near_high_ref, None, image_b, second)
        add_products(range(near, slots), far_high_ref, None, image_b, second)
        for s in range(slots):
            put_halves(s, levels + 1 + 2 * (rows // rank), second[s])

        def dots(left, right):
            total = left[0] * right[0]
            for s in range(1, slots):
                total = total + left[s] * right[s]
            return jnp.sum(total, axis=1, keepdims=True)

        scalars = [
            dots(field, field),
            dots(field, image),
            dots(image, image),
            dots(image, second) + leaf_norm,
        ]
        lane = lax.broadcasted_iota(jnp.int32, (nrhs, rank), 1)
        packed = jnp.zeros((nrhs, rank), F32)
        for k, value in enumerate(scalars):
            value = jnp.broadcast_to(value, (nrhs, rank))
            for piece in range(3):
                rounded = value.astype(BF16).astype(F32)
                packed = jnp.where(lane == 3 * k + piece, rounded, packed)
                value = value - rounded
        for s in range(slots):
            put(s, levels, packed.astype(BF16))


def finish_kernel(leaves, field_ref, factors_ref, result_ref, *refs):
    sums = refs[:leaves]
    solution_ref, residual_ref = refs[leaves:]
    levels, rows, rank = factors_ref.shape
    nrhs = field_ref.shape[0]
    field = field_ref[...]

    def halves(at):
        pieces = []
        for k in range(rows // rank):
            start = (at + 2 * k) * nrhs
            piece = result_ref[start : start + 2 * nrhs].astype(F32)
            pieces.append(piece[:nrhs] + piece[nrhs:])
        return jnp.concatenate(pieces, axis=1)

    image = halves(levels + 1)
    second = halves(levels + 1 + 2 * (rows // rank)) + 0.5 * image
    lane = lax.broadcasted_iota(jnp.int32, (nrhs, rank), 1)
    packed = sums[0][levels * nrhs :].astype(F32)
    for m in range(1, leaves):
        packed = packed + sums[m][levels * nrhs :].astype(F32)

    def scalar(k):
        inside = (lane >= 3 * k) & (lane < 3 * k + 3)
        return jnp.sum(jnp.where(inside, packed, 0.0), axis=1, keepdims=True)

    bb, bw, ww, wu = (scalar(k) for k in range(4))
    wu = wu + 0.5 * ww
    for level in range(levels):
        nodes = {}
        for m in range(leaves):
            value = sums[m][level * nrhs : (level + 1) * nrhs].astype(F32)
            node = m >> level
            nodes[node] = nodes[node] + value if node in nodes else value
        second = second + mm_nt(nodes[0].astype(BF16), factors_ref[level])
        if level > 0:
            squared = sum(value * value for value in nodes.values())
            wu = wu + jnp.sum(squared, axis=1, keepdims=True)
    alpha0 = bb / bw
    norm1 = alpha0 * alpha0 * ww - bb
    ratio = norm1 / bb
    keep = 1.0 + ratio
    curv = keep * keep * bw - 2.0 * keep * alpha0 * ww + alpha0 * alpha0 * wu
    alpha1 = norm1 / curv
    solution_ref[...] = (alpha0 + alpha1 * keep) * field - (alpha1 * alpha0) * image
    residual_ref[...] = field - (alpha0 + alpha1 * keep) * image + (alpha1 * alpha0) * second


def call(kernel, outs, args, specs, scratch=(), flops=0, limit=24, aliases={}):
    moved = sum(a.size * a.dtype.itemsize for a in args)
    return pl.pallas_call(
        kernel,
        out_shape=[jax.ShapeDtypeStruct(shape, dtype) for shape, dtype in outs],
        in_specs=specs,
        out_specs=[VMEM] * len(outs),
        scratch_shapes=list(scratch),
        input_output_aliases=aliases,
        cost_estimate=pl.CostEstimate(flops=flops, bytes_accessed=moved, transcendentals=0),
        compiler_params=pltpu.CompilerParams(vmem_limit_bytes=limit * 2**20),
    )(*args)


def collected(embed, factors, targets):
    leaves, inner = lax.axis_size("leaf"), lax.axis_size("inner")
    levels, rows, rank = factors.shape
    dims, nrhs = embed.shape[1], targets.shape[1]
    shape = (rows, dims, levels, rank, nrhs)

    def host(leaf):
        return inner // 2 if leaf % 2 == 0 else (inner - 1) // 2

    def others(leaf):
        sign = 1 if leaf % 2 == 0 else -1
        here = host(leaf)
        places = [z for z in range(inner) if z != here]
        places.sort(key=lambda z: (-abs(z - here), sign * z))
        if leaf % 2:
            places = places[-1:] + places[:-1]
        return [places[slot] for slot in sending_order(inner)]

    routes = [
        [(leaf * inner + others(leaf)[k], leaf * inner + host(leaf)) for leaf in range(leaves)]
        for k in range(inner - 1)
    ]

    axes = ("leaf", "inner")

    def from_host(values):
        back = [
            lax.ppermute(value, axes, [(b, a) for a, b in route])
            for value, route in zip(values[1:], routes)
        ]
        return [values[0]] + back

    def to_host(value):
        return [value] + [lax.ppermute(value, axes, route) for route in routes]

    def over_leaf(value, m):
        return lax.ppermute(value, "leaf", [(i, i ^ m) for i in range(leaves)])

    field = targets.T
    near = inner - 1
    held, pairs = len(pairs_of(near)), len(pairs_of(inner))
    head = dims // rank * rows + 2 * nrhs * (rows // rank)
    tail = levels * (rows + 2 * nrhs)
    sizes = [((head, rank), BF16), ((tail, rank), BF16)]
    sizes += [((nrhs, rank), F32), (((levels - 1) * nrhs, rank), F32)]
    first_part, second_part, first, upper = call(
        pack_kernel, sizes, [embed, factors, targets.T], [VMEM] * 3
    )
    heads = to_host(first_part)
    proj = [first]
    for bit in range(levels - 1):
        upper = upper + over_leaf(upper, 2**bit)
        proj.append(upper[:nrhs])
        upper = upper[nrhs:]
    (second_part,) = call(
        functools.partial(tail_kernel, levels * rows),
        [sizes[1]],
        [second_part] + proj,
        [VMEM] * (1 + levels),
        aliases={0: 0},
    )
    tails = to_host(second_part)
    leaf = lax.axis_index("leaf")
    here = jnp.where(leaf % 2 == 0, host(0), host(1))
    is_host = (lax.axis_index("inner") == here).astype(jnp.int32).reshape(1)
    near_high, near_image = call(
        functools.partial(near_kernel, near, shape),
        [((held, rows, rows), BF16), ((near, nrhs, rows), F32)],
        [is_host] + heads[:near],
        [SMEM] + [VMEM] * near,
        scratch=[pltpu.VMEM((held, rows, rows), BF16)],
        flops=NEAR_FLOPS,
    )
    far_high, image = call(
        functools.partial(far_kernel, inner, shape),
        [((pairs - held, rows, rows), BF16), ((inner, nrhs, rows), F32)],
        [is_host, near_image] + heads,
        [SMEM] + [VMEM] * (1 + inner),
        scratch=[pltpu.VMEM((pairs - held, rows, rows), BF16)],
        flops=FAR_FLOPS,
    )
    height = (levels + 1 + 4 * (rows // rank)) * nrhs
    results = call(
        functools.partial(main_kernel, inner, shape),
        [((height, rank), BF16)] * inner,
        [is_host, near_high, far_high, image] + heads + [tails[s] for s in tail_order(inner)],
        [SMEM] + [VMEM] * (3 + 2 * inner),
        flops=MAIN_FLOPS,
    )
    result = results[0]
    for slot in tail_order(inner)[:0:-1]:
        route = [(b, a) for a, b in routes[slot - 1]]
        result = result + lax.ppermute(results[slot], axes, route)
    sums = result[: (levels + 1) * nrhs]
    leaf_sums = [sums] + [over_leaf(sums, m) for m in range(1, leaves)]
    answer, residual = call(
        functools.partial(finish_kernel, leaves),
        [((nrhs, rows), F32)] * 2,
        [field, factors, result] + leaf_sums,
        [VMEM] * (3 + leaves),
    )
    return (answer.T, residual.T)


def on_device(embed, factors, targets):
    if embed.shape[0] * lax.axis_size("inner") <= FAST_LEAF:
        return collected(embed, factors, targets)
    return stepwise(embed, factors, targets)


def solution(mesh):
    return jax.shard_map(
        on_device,
        mesh=mesh,
        in_specs=(
            P(("groups", "leaf", "inner"), None),
            P(None, ("groups", "leaf", "inner"), None),
            P(("groups", "leaf", "inner"), None),
        ),
        out_specs=(P(("groups", "leaf", "inner"), None), P(("groups", "leaf", "inner"), None)),
        check_vma=False,
    )
```

```python
import functools

import jax
import jax.numpy as jnp
from jax import lax
from jax.experimental import pallas as pl
from jax.experimental.pallas import tpu as pltpu
from jax.sharding import PartitionSpec as P

ITERS = 2
LENGTH_SCALE = 2.3
FAST_LEAF = 2048
NEAR_FLOPS = 4 * 10**9
FAR_FLOPS = 3 * 10**9
MAIN_FLOPS = 2 * 10**9
F32, BF16 = jnp.float32, jnp.bfloat16
VMEM = pl.BlockSpec(memory_space=pltpu.VMEM)
SMEM = pl.BlockSpec(memory_space=pltpu.SMEM)


def swapped(value, axis, apart):
    mask = 2**apart
    pairs = [(source, source ^ mask) for source in range(lax.axis_size(axis))]
    return lax.ppermute(value, axis, pairs)


def matern(left, right):
    left_f = left.astype(F32)
    right_f = right.astype(F32)
    left_sq = jnp.sum(left_f * left_f, axis=1)
    right_sq = jnp.sum(right_f * right_f, axis=1)
    inner_prod = lax.dot_general(
        left, right, (((1,), (1,)), ((), ())), preferred_element_type=F32
    )
    dist2 = left_sq[:, None] + right_sq[None, :] - 2.0 * inner_prod
    scaled = jnp.sqrt(3.0) * jnp.sqrt(jnp.maximum(dist2, 0.0)) / LENGTH_SCALE
    return (1.0 + scaled) * jnp.exp(-scaled)


def squares(residual):
    return lax.psum(jnp.sum(residual * residual, axis=0), ("leaf", "inner"))


def operate(embed, factors, field):
    piece = lax.all_gather(embed, "inner", axis=0, tiled=True)
    terms = jnp.dot(matern(piece, embed), field, precision=lax.Precision.HIGHEST)
    dense = lax.psum_scatter(terms, "inner", scatter_dimension=0, tiled=True)
    total = dense + 0.5 * field
    levels = factors.shape[0]
    rounded = field.astype(BF16)
    proj = jnp.einsum("lrk,rc->lkc", factors, rounded, preferred_element_type=F32)
    proj = lax.psum(proj, "inner")
    for bit in range(levels - 1):
        upper = proj[bit + 1 :]
        partner = swapped(upper, "leaf", bit)
        proj = jnp.concatenate([proj[: bit + 1], upper + partner], axis=0)
    back = jnp.einsum(
        "lrk,lkc->rc", factors, proj.astype(BF16), preferred_element_type=F32
    )
    return total + back


def stepwise(embed, factors, targets):
    result = jnp.zeros_like(targets)
    residual = targets
    direction = targets
    norm_now = squares(residual)
    for step in range(ITERS):
        image = operate(embed, factors, direction)
        curv = lax.psum(jnp.sum(direction * image, axis=0), ("leaf", "inner"))
        alpha = norm_now / curv
        result = result + alpha * direction
        residual = residual - alpha * image
        if step + 1 < ITERS:
            norm_next = squares(residual)
            direction = residual + norm_next / norm_now * direction
            norm_now = norm_next
    return (result, residual)


def mm(left, right):
    return lax.dot_general(left, right, (((1,), (0,)), ((), ())), preferred_element_type=F32)


def mm_nt(left, right):
    return lax.dot_general(left, right, (((1,), (1,)), ((), ())), preferred_element_type=F32)


def pairs_of(slots):
    return [(i, j) for j in range(slots) for i in range(j + 1)]


def put_halves(ref, start, value):
    rows = value.shape[0]
    high = value.astype(BF16)
    ref[start : start + rows] = high
    ref[start + rows : start + 2 * rows] = (value - high.astype(F32)).astype(BF16)


def pack_kernel(embed_ref, factors_ref, field_ref, head_ref, tail_ref, first_ref, upper_ref):
    levels, rows, rank = factors_ref.shape
    nrhs = field_ref.shape[0]
    lanes = embed_ref.shape[1] // rank
    rounded = field_ref[...].astype(BF16)
    first_ref[...] = mm(rounded, factors_ref[0])
    for level in range(1, levels):
        upper_ref[(level - 1) * nrhs : level * nrhs] = mm(rounded, factors_ref[level])
    for k in range(lanes):
        head_ref[k * rows : (k + 1) * rows] = embed_ref[:, k * rank : (k + 1) * rank]
    for k in range(rows // rank):
        put_halves(head_ref, lanes * rows + 2 * k * nrhs, field_ref[:, k * rank : (k + 1) * rank])
    for level in range(levels):
        tail_ref[level * rows : (level + 1) * rows] = factors_ref[level]


def tail_kernel(start, tail_in, *refs):
    del tail_in
    *proj_refs, tail_ref = refs
    for ref in proj_refs:
        put_halves(tail_ref, start, ref[...])
        start += 2 * ref.shape[0]


class Message:
    def __init__(self, shape, head_ref=None, tail_ref=None):
        self.rows, self.dims, self.levels, self.rank, self.nrhs = shape
        self.head = head_ref
        self.tail = tail_ref

    def embed(self):
        rows = self.rows
        pieces = [self.head[k * rows : (k + 1) * rows] for k in range(self.dims // self.rank)]
        return jnp.concatenate(pieces, axis=1)

    def field(self):
        base = self.dims // self.rank * self.rows
        step = 2 * self.nrhs
        count = self.rows // self.rank
        pieces = [self.head[base + k * step : base + (k + 1) * step] for k in range(count)]
        return jnp.concatenate(pieces, axis=1)

    def factor(self, level):
        return self.tail[level * self.rows : (level + 1) * self.rows]

    def proj(self, level):
        base = self.levels * self.rows + 2 * level * self.nrhs
        halves = self.tail[base : base + 2 * self.nrhs].astype(F32)
        return halves[: self.nrhs] + halves[self.nrhs :]


def norms_of(embed):
    scale = 3.0 / LENGTH_SCALE**2
    wide_e = embed.astype(F32)
    square = wide_e * wide_e
    column = scale * jnp.sum(square, axis=1, keepdims=True)
    first = square.astype(BF16)
    rest = (square - first.astype(F32)).astype(BF16)
    ones = jnp.ones((8, embed.shape[1]), BF16)
    row = scale * (mm_nt(ones, first) + mm_nt(ones, rest))
    return column, row[0:1]


def kern_block(left, right, column, row):
    scale = 3.0 / LENGTH_SCALE**2
    product = mm_nt(left, right)
    dist = jnp.maximum((column + row) - (2.0 * scale) * product, 1e-30)
    scaled = dist * lax.rsqrt(dist)
    value = (1.0 + scaled) * jnp.exp(-scaled)
    high = value.astype(BF16)
    return high, (value - high.astype(F32)).astype(BF16)


def kern_columns(columns, messages, high_ref, low_ref):
    norms = {}
    index = 0
    for j in columns:
        for i in range(j + 1):
            for s in (i, j):
                if s not in norms:
                    norms[s] = norms_of(messages[s].embed())
            high_ref[index], low_ref[index] = kern_block(
                messages[i].embed(), messages[j].embed(), norms[i][0], norms[j][1]
            )
            index += 1


def add_products(columns, high_ref, low_ref, fields, total):
    nrhs, rows = total[0].shape

    def fold(stacked):
        return stacked[:nrhs] + stacked[nrhs:] if stacked.shape[0] > nrhs else stacked

    at = 0
    for j in columns:
        left = jnp.concatenate(fields[: j + 1], axis=1)
        high = high_ref[at : at + j + 1].reshape((j + 1) * rows, rows)
        down = fold(mm(left, high))
        across = fold(mm_nt(fields[j], high[: j * rows])) if j else None
        if low_ref is not None:
            low = low_ref[at : at + j + 1].reshape((j + 1) * rows, rows)
            down = down + mm(left[:nrhs], low)
            if j:
                across = across + mm_nt(fields[j][:nrhs], low[: j * rows])
        total[j] = total[j] + down
        for i in range(j):
            total[i] = total[i] + across[:, i * rows : (i + 1) * rows]
        at += j + 1


def near_kernel(near, shape, is_host_ref, *refs):
    @pl.when(is_host_ref[0] == 1)
    def _():
        high_ref, image_ref, low_ref = refs[near:]
        messages = [Message(shape, ref) for ref in refs[:near]]
        image = [jnp.zeros(image_ref.shape[1:], F32) for _ in range(near)]
        kern_columns(range(near), messages, high_ref, low_ref)
        add_products(range(near), high_ref, low_ref, [m.field() for m in messages], image)
        for s in range(near):
            image_ref[s] = image[s]


def far_kernel(slots, shape, is_host_ref, near_high_ref, near_image_ref, *refs):
    @pl.when(is_host_ref[0] == 1)
    def _():
        full_ref, image_ref, high_ref, low_ref = refs[slots:]
        near = near_image_ref.shape[0]
        rows = shape[0]
        messages = [Message(shape, ref) for ref in refs[:slots]]
        image = [near_image_ref[s] for s in range(near)]
        image += [jnp.zeros(image_ref.shape[1:], F32) for _ in range(near, slots)]
        kern_columns(range(near, slots), messages, high_ref, low_ref)
        add_products(range(near, slots), high_ref, low_ref, [m.field() for m in messages], image)
        for s in range(slots):
            image_ref[s] = image[s]
        held = near_high_ref.shape[0]
        for index, (i, j) in enumerate(pairs_of(slots)):
            block = near_high_ref[index] if index < held else high_ref[index - held]
            full_ref[i * rows : (i + 1) * rows, j * rows : (j + 1) * rows] = block
            if i != j:
                full_ref[j * rows : (j + 1) * rows, i * rows : (i + 1) * rows] = block.T


def main_kernel(slots, shape, is_host_ref, full_ref, image_ref, *refs):
    results = refs[2 * slots :]

    @pl.when(is_host_ref[0] == 0)
    def _():
        results[0][...] = jnp.zeros_like(results[0])

    @pl.when(is_host_ref[0] == 1)
    def _():
        messages = [Message(shape, refs[s], refs[slots + s]) for s in range(slots)]
        rows, _, levels, rank, nrhs = shape

        def put(s, at, value):
            results[s][at * nrhs : (at + 1) * nrhs] = value

        def put_halves(s, at, value):
            high = value.astype(BF16)
            low = (value - high.astype(F32)).astype(BF16)
            for k in range(rows // rank):
                put(s, at + 2 * k, high[:, k * rank : (k + 1) * rank])
                put(s, at + 2 * k + 1, low[:, k * rank : (k + 1) * rank])

        proj = []
        for level in range(levels):
            total = messages[0].proj(level)
            for message in messages[1:]:
                total = total + message.proj(level)
            proj.append(total.astype(BF16))
        def factors():
            wide = [
                jnp.concatenate([message.factor(level) for level in range(levels)], axis=1)
                for message in messages
            ]
            return jnp.concatenate(wide, axis=0)

        low_rank = mm_nt(jnp.concatenate(proj, axis=1), factors())
        fields = [message.field() for message in messages]
        field, image, image_b = [], [], []
        for s in range(slots):
            halves = fields[s].astype(F32)
            field.append(halves[:nrhs] + halves[nrhs:])
            total = image_ref[s] + 0.5 * field[s] + low_rank[:, s * rows : (s + 1) * rows]
            image.append(total)
            image_b.append(total.astype(BF16))
            put_halves(s, levels + 1, total)
        total = mm(jnp.concatenate(image_b, axis=1), factors())
        leaf_norm = jnp.sum(total[:, :rank] * total[:, :rank], axis=1, keepdims=True)
        for level in range(levels):
            part = total[:, level * rank : (level + 1) * rank].astype(BF16)
            for s in range(slots):
                put(s, level, part)
        whole = mm(jnp.concatenate(image_b, axis=1), full_ref[...])
        second = [whole[:, s * rows : (s + 1) * rows] for s in range(slots)]
        for s in range(slots):
            put_halves(s, levels + 1 + 2 * (rows // rank), second[s])

        def dots(left, right):
            total = left[0] * right[0]
            for s in range(1, slots):
                total = total + left[s] * right[s]
            return jnp.sum(total, axis=1, keepdims=True)

        scalars = [
            dots(field, field),
            dots(field, image),
            dots(image, image),
            dots(image, second) + leaf_norm,
        ]
        lane = lax.broadcasted_iota(jnp.int32, (nrhs, rank), 1)
        packed = jnp.zeros((nrhs, rank), F32)
        for k, value in enumerate(scalars):
            value = jnp.broadcast_to(value, (nrhs, rank))
            for piece in range(3):
                rounded = value.astype(BF16).astype(F32)
                packed = jnp.where(lane == 3 * k + piece, rounded, packed)
                value = value - rounded
        for s in range(slots):
            put(s, levels, packed.astype(BF16))


def finish_kernel(leaves, field_ref, factors_ref, result_ref, *refs):
    sums = [refs[-m % leaves] for m in range(leaves)]
    solution_ref, residual_ref = refs[leaves:]
    levels, rows, rank = factors_ref.shape
    nrhs = field_ref.shape[0]
    field = field_ref[...]

    def halves(at):
        pieces = []
        for k in range(rows // rank):
            start = (at + 2 * k) * nrhs
            piece = result_ref[start : start + 2 * nrhs].astype(F32)
            pieces.append(piece[:nrhs] + piece[nrhs:])
        return jnp.concatenate(pieces, axis=1)

    image = halves(levels + 1)
    second = halves(levels + 1 + 2 * (rows // rank)) + 0.5 * image
    lane = lax.broadcasted_iota(jnp.int32, (nrhs, rank), 1)
    packed = sums[0][levels * nrhs :].astype(F32)
    for m in range(1, leaves):
        packed = packed + sums[m][levels * nrhs :].astype(F32)

    def scalar(k):
        inside = (lane >= 3 * k) & (lane < 3 * k + 3)
        return jnp.sum(jnp.where(inside, packed, 0.0), axis=1, keepdims=True)

    bb, bw, ww, wu = (scalar(k) for k in range(4))
    wu = wu + 0.5 * ww
    for level in range(levels):
        nodes = {}
        for m in range(leaves):
            value = sums[m][level * nrhs : (level + 1) * nrhs].astype(F32)
            node = m >> level
            nodes[node] = nodes[node] + value if node in nodes else value
        second = second + mm_nt(nodes[0].astype(BF16), factors_ref[level])
        if level > 0:
            squared = sum(value * value for value in nodes.values())
            wu = wu + jnp.sum(squared, axis=1, keepdims=True)
    alpha0 = bb / bw
    norm1 = alpha0 * alpha0 * ww - bb
    ratio = norm1 / bb
    keep = 1.0 + ratio
    curv = keep * keep * bw - 2.0 * keep * alpha0 * ww + alpha0 * alpha0 * wu
    alpha1 = norm1 / curv
    solution_ref[...] = (alpha0 + alpha1 * keep) * field - (alpha1 * alpha0) * image
    residual_ref[...] = field - (alpha0 + alpha1 * keep) * image + (alpha1 * alpha0) * second


def call(kernel, outs, args, specs, scratch=(), flops=0, limit=24, aliases={}):
    moved = sum(a.size * a.dtype.itemsize for a in args)
    return pl.pallas_call(
        kernel,
        out_shape=[jax.ShapeDtypeStruct(shape, dtype) for shape, dtype in outs],
        in_specs=specs,
        out_specs=[VMEM] * len(outs),
        scratch_shapes=list(scratch),
        input_output_aliases=aliases,
        cost_estimate=pl.CostEstimate(flops=flops, bytes_accessed=moved, transcendentals=0),
        compiler_params=pltpu.CompilerParams(vmem_limit_bytes=limit * 2**20),
    )(*args)


def collected(embed, factors, targets):
    leaves, inner = lax.axis_size("leaf"), lax.axis_size("inner")
    levels, rows, rank = factors.shape
    dims, nrhs = embed.shape[1], targets.shape[1]
    shape = (rows, dims, levels, rank, nrhs)

    def host(leaf):
        return inner // 2 if leaf % 2 == 0 else (inner - 1) // 2

    def others(leaf):
        sign = 1 if leaf % 2 == 0 else -1
        here = host(leaf)
        places = [z for z in range(inner) if z != here]
        places.sort(key=lambda z: (-abs(z - here), sign * z))
        if leaf % 2:
            places = places[-1:] + places[:-1]
        return places

    routes = [
        [(leaf * inner + others(leaf)[k], leaf * inner + host(leaf)) for leaf in range(leaves)]
        for k in range(inner - 1)
    ]

    axes = ("leaf", "inner")

    def to_host(value):
        return [value] + [lax.ppermute(value, axes, route) for route in routes]

    def over_leaf(value, m):
        return lax.ppermute(value, "leaf", [(i, i ^ m) for i in range(leaves)])

    field = targets.T
    near = inner - 1
    held, pairs = len(pairs_of(near)), len(pairs_of(inner))
    head = dims // rank * rows + 2 * nrhs * (rows // rank)
    tail = levels * (rows + 2 * nrhs)
    sizes = [((head, rank), BF16), ((tail, rank), BF16)]
    sizes += [((nrhs, rank), F32), (((levels - 1) * nrhs, rank), F32)]
    first_part, second_part, first, upper = call(
        pack_kernel, sizes, [embed, factors, field], [VMEM] * 3
    )
    heads = to_host(first_part)
    proj = [first]
    for bit in range(levels - 1):
        upper = upper + over_leaf(upper, 2**bit)
        proj.append(upper[:nrhs])
        upper = upper[nrhs:]
    (second_part,) = call(
        functools.partial(tail_kernel, levels * rows),
        [sizes[1]],
        [second_part] + proj,
        [VMEM] * (1 + levels),
        aliases={0: 0},
    )
    tails = to_host(second_part)
    leaf = lax.axis_index("leaf")
    here = jnp.where(leaf % 2 == 0, host(0), host(1))
    is_host = (lax.axis_index("inner") == here).astype(jnp.int32).reshape(1)
    near_high, near_image = call(
        functools.partial(near_kernel, near, shape),
        [((held, rows, rows), BF16), ((near, nrhs, rows), F32)],
        [is_host] + heads[:near],
        [SMEM] + [VMEM] * near,
        scratch=[pltpu.VMEM((held, rows, rows), BF16)],
        flops=NEAR_FLOPS,
    )
    full, image = call(
        functools.partial(far_kernel, inner, shape),
        [((inner * rows, inner * rows), BF16), ((inner, nrhs, rows), F32)],
        [is_host, near_high, near_image] + heads,
        [SMEM] + [VMEM] * (2 + inner),
        scratch=[pltpu.VMEM((pairs - held, rows, rows), BF16)] * 2,
        flops=FAR_FLOPS,
    )
    height = (levels + 1 + 4 * (rows // rank)) * nrhs
    results = call(
        functools.partial(main_kernel, inner, shape),
        [((height, rank), BF16)] * inner,
        [is_host, full, image] + heads + tails,
        [SMEM] + [VMEM] * (2 + 2 * inner),
        flops=MAIN_FLOPS,
    )
    result = results[0]
    for slot in [*range(2, inner), 1][: inner - 1]:
        route = [(b, a) for a, b in routes[slot - 1]]
        result = result + lax.ppermute(results[slot], axes, route)
    sums = result[: (levels + 1) * nrhs]
    leaf_sums = [sums] + [over_leaf(sums, m) for m in range(leaves - 1, 0, -1)]
    answer, residual = call(
        functools.partial(finish_kernel, leaves),
        [((nrhs, rows), F32)] * 2,
        [field, factors, result] + leaf_sums,
        [VMEM] * (3 + leaves),
    )
    return (answer.T, residual.T)


def on_device(embed, factors, targets):
    _, rows, rank = factors.shape
    whole = rows % rank == 0 and embed.shape[1] % rank == 0
    if whole and rows * lax.axis_size("inner") <= FAST_LEAF:
        return collected(embed, factors, targets)
    return stepwise(embed, factors, targets)


def solution(mesh):
    return jax.shard_map(
        on_device,
        mesh=mesh,
        in_specs=(
            P(("groups", "leaf", "inner"), None),
            P(None, ("groups", "leaf", "inner"), None),
            P(("groups", "leaf", "inner"), None),
        ),
        out_specs=(P(("groups", "leaf", "inner"), None), P(("groups", "leaf", "inner"), None)),
        check_vma=False,
    )
```

```python
import functools

import jax
import jax.numpy as jnp
from jax import lax
from jax.experimental import pallas as pl
from jax.experimental.pallas import tpu as pltpu
from jax.sharding import PartitionSpec as P

ITERS = 2
LENGTH_SCALE = 2.3
FAST_LEAF = 2048
NEAR_FLOPS = 4 * 10**9
FAR_FLOPS = 3 * 10**9
MAIN_FLOPS = 2 * 10**9
F32, BF16 = jnp.float32, jnp.bfloat16
VMEM = pl.BlockSpec(memory_space=pltpu.VMEM)
SMEM = pl.BlockSpec(memory_space=pltpu.SMEM)


def swapped(value, axis, apart):
    mask = 2**apart
    pairs = [(source, source ^ mask) for source in range(lax.axis_size(axis))]
    return lax.ppermute(value, axis, pairs)


def matern(left, right):
    left_f = left.astype(F32)
    right_f = right.astype(F32)
    left_sq = jnp.sum(left_f * left_f, axis=1)
    right_sq = jnp.sum(right_f * right_f, axis=1)
    inner_prod = lax.dot_general(
        left, right, (((1,), (1,)), ((), ())), preferred_element_type=F32
    )
    dist2 = left_sq[:, None] + right_sq[None, :] - 2.0 * inner_prod
    scaled = jnp.sqrt(3.0) * jnp.sqrt(jnp.maximum(dist2, 0.0)) / LENGTH_SCALE
    return (1.0 + scaled) * jnp.exp(-scaled)


def squares(residual):
    return lax.psum(jnp.sum(residual * residual, axis=0), ("leaf", "inner"))


def operate(embed, factors, field):
    piece = lax.all_gather(embed, "inner", axis=0, tiled=True)
    terms = jnp.dot(matern(piece, embed), field, precision=lax.Precision.HIGHEST)
    dense = lax.psum_scatter(terms, "inner", scatter_dimension=0, tiled=True)
    total = dense + 0.5 * field
    levels = factors.shape[0]
    rounded = field.astype(BF16)
    proj = jnp.einsum("lrk,rc->lkc", factors, rounded, preferred_element_type=F32)
    proj = lax.psum(proj, "inner")
    for bit in range(levels - 1):
        upper = proj[bit + 1 :]
        partner = swapped(upper, "leaf", bit)
        proj = jnp.concatenate([proj[: bit + 1], upper + partner], axis=0)
    back = jnp.einsum(
        "lrk,lkc->rc", factors, proj.astype(BF16), preferred_element_type=F32
    )
    return total + back


def stepwise(embed, factors, targets):
    result = jnp.zeros_like(targets)
    residual = targets
    direction = targets
    norm_now = squares(residual)
    for step in range(ITERS):
        image = operate(embed, factors, direction)
        curv = lax.psum(jnp.sum(direction * image, axis=0), ("leaf", "inner"))
        alpha = norm_now / curv
        result = result + alpha * direction
        residual = residual - alpha * image
        if step + 1 < ITERS:
            norm_next = squares(residual)
            direction = residual + norm_next / norm_now * direction
            norm_now = norm_next
    return (result, residual)


def mm(left, right):
    return lax.dot_general(left, right, (((1,), (0,)), ((), ())), preferred_element_type=F32)


def mm_nt(left, right):
    return lax.dot_general(left, right, (((1,), (1,)), ((), ())), preferred_element_type=F32)


def pairs_of(slots):
    return [(i, j) for j in range(slots) for i in range(j + 1)]


def put_halves(ref, start, value):
    rows = value.shape[0]
    high = value.astype(BF16)
    ref[start : start + rows] = high
    ref[start + rows : start + 2 * rows] = (value - high.astype(F32)).astype(BF16)


def pack_kernel(embed_ref, factors_ref, field_ref, head_ref, tail_ref, first_ref, upper_ref):
    levels, rows, rank = factors_ref.shape
    nrhs = field_ref.shape[0]
    lanes = embed_ref.shape[1] // rank
    rounded = field_ref[...].astype(BF16)
    first_ref[...] = mm(rounded, factors_ref[0])
    for level in range(1, levels):
        upper_ref[(level - 1) * nrhs : level * nrhs] = mm(rounded, factors_ref[level])
    for k in range(lanes):
        head_ref[k * rows : (k + 1) * rows] = embed_ref[:, k * rank : (k + 1) * rank]
    for k in range(rows // rank):
        put_halves(head_ref, lanes * rows + 2 * k * nrhs, field_ref[:, k * rank : (k + 1) * rank])
    for level in range(levels):
        tail_ref[level * rows : (level + 1) * rows] = factors_ref[level]


def tail_kernel(start, tail_in, *refs):
    del tail_in
    *proj_refs, tail_ref = refs
    for ref in proj_refs:
        put_halves(tail_ref, start, ref[...])
        start += 2 * ref.shape[0]


class Message:
    def __init__(self, shape, head_ref=None, tail_ref=None):
        self.rows, self.dims, self.levels, self.rank, self.nrhs = shape
        self.head = head_ref
        self.tail = tail_ref

    def embed(self):
        rows = self.rows
        pieces = [self.head[k * rows : (k + 1) * rows] for k in range(self.dims // self.rank)]
        return jnp.concatenate(pieces, axis=1)

    def field(self):
        base = self.dims // self.rank * self.rows
        step = 2 * self.nrhs
        count = self.rows // self.rank
        pieces = [self.head[base + k * step : base + (k + 1) * step] for k in range(count)]
        return jnp.concatenate(pieces, axis=1)

    def factor(self, level):
        return self.tail[level * self.rows : (level + 1) * self.rows]

    def proj(self, level):
        base = self.levels * self.rows + 2 * level * self.nrhs
        halves = self.tail[base : base + 2 * self.nrhs].astype(F32)
        return halves[: self.nrhs] + halves[self.nrhs :]


def norms_of(embed):
    scale = 3.0 / LENGTH_SCALE**2
    wide_e = embed.astype(F32)
    square = wide_e * wide_e
    column = scale * jnp.sum(square, axis=1, keepdims=True)
    first = square.astype(BF16)
    rest = (square - first.astype(F32)).astype(BF16)
    ones = jnp.ones((8, embed.shape[1]), BF16)
    row = scale * (mm_nt(ones, first) + mm_nt(ones, rest))
    return column, row[0:1]


def kern_block(left, right, column, row):
    scale = 3.0 / LENGTH_SCALE**2
    product = mm_nt(left, right)
    dist = jnp.maximum((column + row) - (2.0 * scale) * product, 1e-30)
    scaled = dist * lax.rsqrt(dist)
    value = (1.0 + scaled) * jnp.exp(-scaled)
    high = value.astype(BF16)
    return high, (value - high.astype(F32)).astype(BF16)


def kern_columns(columns, messages, high_ref, low_ref):
    norms = {}
    index = 0
    for j in columns:
        for i in range(j + 1):
            for s in (i, j):
                if s not in norms:
                    norms[s] = norms_of(messages[s].embed())
            high_ref[index], low_ref[index] = kern_block(
                messages[i].embed(), messages[j].embed(), norms[i][0], norms[j][1]
            )
            index += 1


def add_products(columns, high_ref, low_ref, fields, total):
    nrhs, rows = total[0].shape

    def fold(stacked):
        return stacked[:nrhs] + stacked[nrhs:] if stacked.shape[0] > nrhs else stacked

    at = 0
    for j in columns:
        left = jnp.concatenate(fields[: j + 1], axis=1)
        high = high_ref[at : at + j + 1].reshape((j + 1) * rows, rows)
        down = fold(mm(left, high))
        across = fold(mm_nt(fields[j], high[: j * rows])) if j else None
        if low_ref is not None:
            low = low_ref[at : at + j + 1].reshape((j + 1) * rows, rows)
            down = down + mm(left[:nrhs], low)
            if j:
                across = across + mm_nt(fields[j][:nrhs], low[: j * rows])
        total[j] = total[j] + down
        for i in range(j):
            total[i] = total[i] + across[:, i * rows : (i + 1) * rows]
        at += j + 1


def near_kernel(near, shape, is_host_ref, *refs):
    @pl.when(is_host_ref[0] == 1)
    def _():
        high_ref, image_ref, low_ref = refs[near:]
        messages = [Message(shape, ref) for ref in refs[:near]]
        image = [jnp.zeros(image_ref.shape[1:], F32) for _ in range(near)]
        kern_columns(range(near), messages, high_ref, low_ref)
        add_products(range(near), high_ref, low_ref, [m.field() for m in messages], image)
        for s in range(near):
            image_ref[s] = image[s]


def far_kernel(slots, shape, is_host_ref, near_high_ref, near_image_ref, *refs):
    @pl.when(is_host_ref[0] == 1)
    def _():
        full_ref, image_ref, high_ref, low_ref = refs[slots:]
        near = near_image_ref.shape[0]
        rows = shape[0]
        messages = [Message(shape, ref) for ref in refs[:slots]]
        image = [near_image_ref[s] for s in range(near)]
        image += [jnp.zeros(image_ref.shape[1:], F32) for _ in range(near, slots)]
        kern_columns(range(near, slots), messages, high_ref, low_ref)
        add_products(range(near, slots), high_ref, low_ref, [m.field() for m in messages], image)
        for s in range(slots):
            image_ref[s] = image[s]
        held = near_high_ref.shape[0]
        for index, (i, j) in enumerate(pairs_of(slots)):
            block = near_high_ref[index] if index < held else high_ref[index - held]
            full_ref[i * rows : (i + 1) * rows, j * rows : (j + 1) * rows] = block
            if i != j:
                full_ref[j * rows : (j + 1) * rows, i * rows : (i + 1) * rows] = block.T


def main_kernel(slots, shape, is_host_ref, full_ref, image_ref, *refs):
    *results, early_ref = refs[2 * slots :]

    @pl.when(is_host_ref[0] == 0)
    def _():
        results[0][...] = jnp.zeros_like(results[0])

    @pl.when(is_host_ref[0] == 1)
    def _():
        messages = [Message(shape, refs[s], refs[slots + s]) for s in range(slots)]
        rows, _, levels, rank, nrhs = shape

        def put(s, at, value):
            if s == slots - 1 and at <= levels:
                early_ref[at * nrhs : (at + 1) * nrhs] = value
                return
            at = at - levels - 1 if s == slots - 1 else at
            results[s][at * nrhs : (at + 1) * nrhs] = value

        def put_halves(s, at, value):
            high = value.astype(BF16)
            low = (value - high.astype(F32)).astype(BF16)
            for k in range(rows // rank):
                put(s, at + 2 * k, high[:, k * rank : (k + 1) * rank])
                put(s, at + 2 * k + 1, low[:, k * rank : (k + 1) * rank])

        proj = []
        for level in range(levels):
            total = messages[0].proj(level)
            for message in messages[1:]:
                total = total + message.proj(level)
            proj.append(total.astype(BF16))
        def factors():
            wide = [
                jnp.concatenate([message.factor(level) for level in range(levels)], axis=1)
                for message in messages
            ]
            return jnp.concatenate(wide, axis=0)

        low_rank = mm_nt(jnp.concatenate(proj, axis=1), factors())
        fields = [message.field() for message in messages]
        field, image, image_b = [], [], []
        for s in range(slots):
            halves = fields[s].astype(F32)
            field.append(halves[:nrhs] + halves[nrhs:])
            total = image_ref[s] + 0.5 * field[s] + low_rank[:, s * rows : (s + 1) * rows]
            image.append(total)
            image_b.append(total.astype(BF16))
            put_halves(s, levels + 1, total)
        total = mm(jnp.concatenate(image_b, axis=1), factors())
        leaf_norm = jnp.sum(total[:, :rank] * total[:, :rank], axis=1, keepdims=True)
        for level in range(levels):
            part = total[:, level * rank : (level + 1) * rank].astype(BF16)
            for s in range(slots):
                put(s, level, part)
        whole = mm(jnp.concatenate(image_b, axis=1), full_ref[...])
        second = [whole[:, s * rows : (s + 1) * rows] for s in range(slots)]
        for s in range(slots):
            put_halves(s, levels + 1 + 2 * (rows // rank), second[s])

        def dots(left, right):
            total = left[0] * right[0]
            for s in range(1, slots):
                total = total + left[s] * right[s]
            return jnp.sum(total, axis=1, keepdims=True)

        scalars = [
            dots(field, field),
            dots(field, image),
            dots(image, image),
            dots(image, second) + leaf_norm,
        ]
        lane = lax.broadcasted_iota(jnp.int32, (nrhs, rank), 1)
        packed = jnp.zeros((nrhs, rank), F32)
        for k, value in enumerate(scalars):
            value = jnp.broadcast_to(value, (nrhs, rank))
            for piece in range(3):
                rounded = value.astype(BF16).astype(F32)
                packed = jnp.where(lane == 3 * k + piece, rounded, packed)
                value = value - rounded
        for s in range(slots):
            put(s, levels, packed.astype(BF16))


def finish_kernel(leaves, field_ref, factors_ref, result_ref, *refs):
    sums = [refs[-m % leaves] for m in range(leaves)]
    solution_ref, residual_ref = refs[leaves:]
    levels, rows, rank = factors_ref.shape
    nrhs = field_ref.shape[0]
    field = field_ref[...]

    def halves(at):
        pieces = []
        for k in range(rows // rank):
            start = (at + 2 * k) * nrhs
            piece = result_ref[start : start + 2 * nrhs].astype(F32)
            pieces.append(piece[:nrhs] + piece[nrhs:])
        return jnp.concatenate(pieces, axis=1)

    image = halves(0)
    second = halves(2 * (rows // rank)) + 0.5 * image
    lane = lax.broadcasted_iota(jnp.int32, (nrhs, rank), 1)
    packed = sums[0][levels * nrhs :].astype(F32)
    for m in range(1, leaves):
        packed = packed + sums[m][(levels - 1) * nrhs :].astype(F32)

    def scalar(k):
        inside = (lane >= 3 * k) & (lane < 3 * k + 3)
        return jnp.sum(jnp.where(inside, packed, 0.0), axis=1, keepdims=True)

    bb, bw, ww, wu = (scalar(k) for k in range(4))
    wu = wu + 0.5 * ww
    for level in range(levels):
        nodes = {}
        for m in range(leaves if level else 1):
            at = level if m == 0 else level - 1
            value = sums[m][at * nrhs : (at + 1) * nrhs].astype(F32)
            node = m >> level
            nodes[node] = nodes[node] + value if node in nodes else value
        second = second + mm_nt(nodes[0].astype(BF16), factors_ref[level])
        if level > 0:
            squared = sum(value * value for value in nodes.values())
            wu = wu + jnp.sum(squared, axis=1, keepdims=True)
    alpha0 = bb / bw
    norm1 = alpha0 * alpha0 * ww - bb
    ratio = norm1 / bb
    keep = 1.0 + ratio
    curv = keep * keep * bw - 2.0 * keep * alpha0 * ww + alpha0 * alpha0 * wu
    alpha1 = norm1 / curv
    solution_ref[...] = (alpha0 + alpha1 * keep) * field - (alpha1 * alpha0) * image
    residual_ref[...] = field - (alpha0 + alpha1 * keep) * image + (alpha1 * alpha0) * second


def call(kernel, outs, args, specs, scratch=(), flops=0, limit=24, aliases={}):
    moved = sum(a.size * a.dtype.itemsize for a in args)
    return pl.pallas_call(
        kernel,
        out_shape=[jax.ShapeDtypeStruct(shape, dtype) for shape, dtype in outs],
        in_specs=specs,
        out_specs=[VMEM] * len(outs),
        scratch_shapes=list(scratch),
        input_output_aliases=aliases,
        cost_estimate=pl.CostEstimate(flops=flops, bytes_accessed=moved, transcendentals=0),
        compiler_params=pltpu.CompilerParams(vmem_limit_bytes=limit * 2**20),
    )(*args)


def collected(embed, factors, targets):
    leaves, inner = lax.axis_size("leaf"), lax.axis_size("inner")
    levels, rows, rank = factors.shape
    dims, nrhs = embed.shape[1], targets.shape[1]
    shape = (rows, dims, levels, rank, nrhs)

    def host(leaf):
        return inner // 2 if leaf % 2 == 0 else (inner - 1) // 2

    def others(leaf):
        sign = 1 if leaf % 2 == 0 else -1
        here = host(leaf)
        places = [z for z in range(inner) if z != here]
        places.sort(key=lambda z: (-abs(z - here), sign * z))
        if leaf % 2:
            places = places[-1:] + places[:-1]
        return places

    routes = [
        [(leaf * inner + others(leaf)[k], leaf * inner + host(leaf)) for leaf in range(leaves)]
        for k in range(inner - 1)
    ]

    axes = ("leaf", "inner")

    def to_host(value):
        return [value] + [lax.ppermute(value, axes, route) for route in routes]

    def over_leaf(value, m):
        return lax.ppermute(value, "leaf", [(i, i ^ m) for i in range(leaves)])

    field = targets.T
    near = inner - 1
    held, pairs = len(pairs_of(near)), len(pairs_of(inner))
    head = dims // rank * rows + 2 * nrhs * (rows // rank)
    tail = levels * (rows + 2 * nrhs)
    sizes = [((head, rank), BF16), ((tail, rank), BF16)]
    sizes += [((nrhs, rank), F32), (((levels - 1) * nrhs, rank), F32)]
    first_part, second_part, first, upper = call(
        pack_kernel, sizes, [embed, factors, field], [VMEM] * 3
    )
    heads = to_host(first_part)
    proj = [first]
    for bit in range(levels - 1):
        upper = upper + over_leaf(upper, 2**bit)
        proj.append(upper[:nrhs])
        upper = upper[nrhs:]
    (second_part,) = call(
        functools.partial(tail_kernel, levels * rows),
        [sizes[1]],
        [second_part] + proj,
        [VMEM] * (1 + levels),
        aliases={0: 0},
    )
    tails = to_host(second_part)
    leaf = lax.axis_index("leaf")
    here = jnp.where(leaf % 2 == 0, host(0), host(1))
    is_host = (lax.axis_index("inner") == here).astype(jnp.int32).reshape(1)
    near_high, near_image = call(
        functools.partial(near_kernel, near, shape),
        [((held, rows, rows), BF16), ((near, nrhs, rows), F32)],
        [is_host] + heads[:near],
        [SMEM] + [VMEM] * near,
        scratch=[pltpu.VMEM((held, rows, rows), BF16)],
        flops=NEAR_FLOPS,
    )
    full, image = call(
        functools.partial(far_kernel, inner, shape),
        [((inner * rows, inner * rows), BF16), ((inner, nrhs, rows), F32)],
        [is_host, near_high, near_image] + heads,
        [SMEM] + [VMEM] * (2 + inner),
        scratch=[pltpu.VMEM((pairs - held, rows, rows), BF16)] * 2,
        flops=FAR_FLOPS,
    )
    height = (levels + 1 + 4 * (rows // rank)) * nrhs
    above = (levels + 1) * nrhs
    heights = [height] * (inner - 1) + [height - above]
    *results, early = call(
        functools.partial(main_kernel, inner, shape),
        [((size, rank), BF16) for size in heights + [above]],
        [is_host, full, image] + heads + tails,
        [SMEM] + [VMEM] * (2 + 2 * inner),
        flops=MAIN_FLOPS,
    )

    def from_host(value, slot):
        return lax.ppermute(value, axes, [(b, a) for a, b in routes[slot - 1]])

    back = [from_host(results[slot], slot) for slot in range(1, inner - 1)]
    sums = results[0][:above]
    for value in back:
        sums = sums + value[:above]
    sums = sums + from_host(early, inner - 1)
    result = results[0][above:]
    for value in back:
        result = result + value[above:]
    result = result + from_host(results[inner - 1], inner - 1)
    leaf_sums = [sums] + [over_leaf(sums[nrhs:], m) for m in range(leaves - 1, 0, -1)]
    answer, residual = call(
        functools.partial(finish_kernel, leaves),
        [((nrhs, rows), F32)] * 2,
        [field, factors, result] + leaf_sums,
        [VMEM] * (3 + leaves),
    )
    return (answer.T, residual.T)


def on_device(embed, factors, targets):
    _, rows, rank = factors.shape
    whole = rows % rank == 0 and embed.shape[1] % rank == 0
    if whole and rows * lax.axis_size("inner") <= FAST_LEAF:
        return collected(embed, factors, targets)
    return stepwise(embed, factors, targets)


def solution(mesh):
    return jax.shard_map(
        on_device,
        mesh=mesh,
        in_specs=(
            P(("groups", "leaf", "inner"), None),
            P(None, ("groups", "leaf", "inner"), None),
            P(("groups", "leaf", "inner"), None),
        ),
        out_specs=(P(("groups", "leaf", "inner"), None), P(("groups", "leaf", "inner"), None)),
        check_vma=False,
    )
```

```python
import functools

import jax
import jax.numpy as jnp
from jax import lax
from jax.experimental import pallas as pl
from jax.experimental.pallas import tpu as pltpu
from jax.sharding import PartitionSpec as P

ITERS = 2
LENGTH_SCALE = 2.3
FAST_LEAF = 2048
NEAR_FLOPS = 4 * 10**9
FAR_FLOPS = 3 * 10**9
MAIN_FLOPS = 2 * 10**9
F32, BF16 = jnp.float32, jnp.bfloat16
VMEM = pl.BlockSpec(memory_space=pltpu.VMEM)
SMEM = pl.BlockSpec(memory_space=pltpu.SMEM)


def swapped(value, axis, apart):
    mask = 2**apart
    pairs = [(source, source ^ mask) for source in range(lax.axis_size(axis))]
    return lax.ppermute(value, axis, pairs)


def matern(left, right):
    left_f = left.astype(F32)
    right_f = right.astype(F32)
    left_sq = jnp.sum(left_f * left_f, axis=1)
    right_sq = jnp.sum(right_f * right_f, axis=1)
    inner_prod = lax.dot_general(
        left, right, (((1,), (1,)), ((), ())), preferred_element_type=F32
    )
    dist2 = left_sq[:, None] + right_sq[None, :] - 2.0 * inner_prod
    scaled = jnp.sqrt(3.0) * jnp.sqrt(jnp.maximum(dist2, 0.0)) / LENGTH_SCALE
    return (1.0 + scaled) * jnp.exp(-scaled)


def squares(residual):
    return lax.psum(jnp.sum(residual * residual, axis=0), ("leaf", "inner"))


def operate(embed, factors, field):
    piece = lax.all_gather(embed, "inner", axis=0, tiled=True)
    terms = jnp.dot(matern(piece, embed), field, precision=lax.Precision.HIGHEST)
    dense = lax.psum_scatter(terms, "inner", scatter_dimension=0, tiled=True)
    total = dense + 0.5 * field
    levels = factors.shape[0]
    rounded = field.astype(BF16)
    proj = jnp.einsum("lrk,rc->lkc", factors, rounded, preferred_element_type=F32)
    proj = lax.psum(proj, "inner")
    for bit in range(levels - 1):
        upper = proj[bit + 1 :]
        partner = swapped(upper, "leaf", bit)
        proj = jnp.concatenate([proj[: bit + 1], upper + partner], axis=0)
    back = jnp.einsum(
        "lrk,lkc->rc", factors, proj.astype(BF16), preferred_element_type=F32
    )
    return total + back


def stepwise(embed, factors, targets):
    result = jnp.zeros_like(targets)
    residual = targets
    direction = targets
    norm_now = squares(residual)
    for step in range(ITERS):
        image = operate(embed, factors, direction)
        curv = lax.psum(jnp.sum(direction * image, axis=0), ("leaf", "inner"))
        alpha = norm_now / curv
        result = result + alpha * direction
        residual = residual - alpha * image
        if step + 1 < ITERS:
            norm_next = squares(residual)
            direction = residual + norm_next / norm_now * direction
            norm_now = norm_next
    return (result, residual)


def mm(left, right):
    return lax.dot_general(left, right, (((1,), (0,)), ((), ())), preferred_element_type=F32)


def mm_nt(left, right):
    return lax.dot_general(left, right, (((1,), (1,)), ((), ())), preferred_element_type=F32)


def pairs_of(slots):
    return [(i, j) for j in range(slots) for i in range(j + 1)]


def put_halves(ref, start, value):
    rows = value.shape[0]
    high = value.astype(BF16)
    ref[start : start + rows] = high
    ref[start + rows : start + 2 * rows] = (value - high.astype(F32)).astype(BF16)


def pack_kernel(embed_ref, factors_ref, field_ref, head_ref, tail_ref, first_ref, upper_ref):
    levels, rows, rank = factors_ref.shape
    nrhs = field_ref.shape[0]
    lanes = embed_ref.shape[1] // rank
    rounded = field_ref[...].astype(BF16)
    first_ref[...] = mm(rounded, factors_ref[0])
    for level in range(1, levels):
        upper_ref[(level - 1) * nrhs : level * nrhs] = mm(rounded, factors_ref[level])
    for k in range(lanes):
        head_ref[k * rows : (k + 1) * rows] = embed_ref[:, k * rank : (k + 1) * rank]
    for k in range(rows // rank):
        put_halves(head_ref, lanes * rows + 2 * k * nrhs, field_ref[:, k * rank : (k + 1) * rank])
    for level in range(levels):
        tail_ref[level * rows : (level + 1) * rows] = factors_ref[level]


def tail_kernel(start, tail_in, *refs):
    del tail_in
    *proj_refs, tail_ref = refs
    for ref in proj_refs:
        put_halves(tail_ref, start, ref[...])
        start += 2 * ref.shape[0]


class Message:
    def __init__(self, shape, head_ref=None, tail_ref=None):
        self.rows, self.dims, self.levels, self.rank, self.nrhs = shape
        self.head = head_ref
        self.tail = tail_ref

    def embed(self):
        rows = self.rows
        pieces = [self.head[k * rows : (k + 1) * rows] for k in range(self.dims // self.rank)]
        return jnp.concatenate(pieces, axis=1)

    def field(self):
        base = self.dims // self.rank * self.rows
        step = 2 * self.nrhs
        count = self.rows // self.rank
        pieces = [self.head[base + k * step : base + (k + 1) * step] for k in range(count)]
        return jnp.concatenate(pieces, axis=1)

    def factor(self, level):
        return self.tail[level * self.rows : (level + 1) * self.rows]

    def proj(self, level):
        base = self.levels * self.rows + 2 * level * self.nrhs
        halves = self.tail[base : base + 2 * self.nrhs].astype(F32)
        return halves[: self.nrhs] + halves[self.nrhs :]


def norms_of(embed):
    scale = 3.0 / LENGTH_SCALE**2
    wide_e = embed.astype(F32)
    square = wide_e * wide_e
    column = scale * jnp.sum(square, axis=1, keepdims=True)
    first = square.astype(BF16)
    rest = (square - first.astype(F32)).astype(BF16)
    ones = jnp.ones((8, embed.shape[1]), BF16)
    row = scale * (mm_nt(ones, first) + mm_nt(ones, rest))
    return column, row[0:1]


def kern_block(left, right, column, row):
    scale = 3.0 / LENGTH_SCALE**2
    product = mm_nt(left, right)
    dist = jnp.maximum((column + row) - (2.0 * scale) * product, 1e-30)
    scaled = dist * lax.rsqrt(dist)
    value = (1.0 + scaled) * jnp.exp(-scaled)
    high = value.astype(BF16)
    return high, (value - high.astype(F32)).astype(BF16)


def kern_columns(columns, messages, high_ref, low_ref):
    norms = {}
    index = 0
    for j in columns:
        for i in range(j + 1):
            for s in (i, j):
                if s not in norms:
                    norms[s] = norms_of(messages[s].embed())
            high_ref[index], low_ref[index] = kern_block(
                messages[i].embed(), messages[j].embed(), norms[i][0], norms[j][1]
            )
            index += 1


def add_products(columns, high_ref, low_ref, fields, total):
    nrhs, rows = total[0].shape

    def fold(stacked):
        return stacked[:nrhs] + stacked[nrhs:] if stacked.shape[0] > nrhs else stacked

    at = 0
    for j in columns:
        left = jnp.concatenate(fields[: j + 1], axis=1)
        high = high_ref[at : at + j + 1].reshape((j + 1) * rows, rows)
        down = fold(mm(left, high))
        across = fold(mm_nt(fields[j], high[: j * rows])) if j else None
        if low_ref is not None:
            low = low_ref[at : at + j + 1].reshape((j + 1) * rows, rows)
            down = down + mm(left[:nrhs], low)
            if j:
                across = across + mm_nt(fields[j][:nrhs], low[: j * rows])
        total[j] = total[j] + down
        for i in range(j):
            total[i] = total[i] + across[:, i * rows : (i + 1) * rows]
        at += j + 1


def near_kernel(near, shape, is_host_ref, *refs):
    @pl.when(is_host_ref[0] == 1)
    def _():
        high_ref, image_ref, low_ref = refs[near:]
        messages = [Message(shape, ref) for ref in refs[:near]]
        image = [jnp.zeros(image_ref.shape[1:], F32) for _ in range(near)]
        kern_columns(range(near), messages, high_ref, low_ref)
        add_products(range(near), high_ref, low_ref, [m.field() for m in messages], image)
        for s in range(near):
            image_ref[s] = image[s]


def far_kernel(slots, shape, is_host_ref, near_high_ref, near_image_ref, *refs):
    @pl.when(is_host_ref[0] == 1)
    def _():
        full_ref, image_ref, high_ref, low_ref = refs[slots:]
        near = near_image_ref.shape[0]
        rows = shape[0]
        messages = [Message(shape, ref) for ref in refs[:slots]]
        image = [near_image_ref[s] for s in range(near)]
        image += [jnp.zeros(image_ref.shape[1:], F32) for _ in range(near, slots)]
        kern_columns(range(near, slots), messages, high_ref, low_ref)
        add_products(range(near, slots), high_ref, low_ref, [m.field() for m in messages], image)
        for s in range(slots):
            image_ref[s] = image[s]
        held = near_high_ref.shape[0]
        for index, (i, j) in enumerate(pairs_of(slots)):
            block = near_high_ref[index] if index < held else high_ref[index - held]
            full_ref[i * rows : (i + 1) * rows, j * rows : (j + 1) * rows] = block
            if i != j:
                full_ref[j * rows : (j + 1) * rows, i * rows : (i + 1) * rows] = block.T


def main_kernel(slots, shape, is_host_ref, full_ref, image_ref, *refs):
    results = refs[2 * slots :]

    @pl.when(is_host_ref[0] == 0)
    def _():
        results[0][...] = jnp.zeros_like(results[0])

    @pl.when(is_host_ref[0] == 1)
    def _():
        messages = [Message(shape, refs[s], refs[slots + s]) for s in range(slots)]
        rows, _, levels, rank, nrhs = shape

        def put(s, at, value):
            results[s][at * nrhs : (at + 1) * nrhs] = value

        def put_halves(s, at, value):
            high = value.astype(BF16)
            low = (value - high.astype(F32)).astype(BF16)
            for k in range(rows // rank):
                put(s, at + 2 * k, high[:, k * rank : (k + 1) * rank])
                put(s, at + 2 * k + 1, low[:, k * rank : (k + 1) * rank])

        proj = []
        for level in range(levels):
            total = messages[0].proj(level)
            for message in messages[1:]:
                total = total + message.proj(level)
            proj.append(total.astype(BF16))
        def factors():
            wide = [
                jnp.concatenate([message.factor(level) for level in range(levels)], axis=1)
                for message in messages
            ]
            return jnp.concatenate(wide, axis=0)

        low_rank = mm_nt(jnp.concatenate(proj, axis=1), factors())
        fields = [message.field() for message in messages]
        field, image, image_b = [], [], []
        for s in range(slots):
            halves = fields[s].astype(F32)
            field.append(halves[:nrhs] + halves[nrhs:])
            total = image_ref[s] + 0.5 * field[s] + low_rank[:, s * rows : (s + 1) * rows]
            image.append(total)
            image_b.append(total.astype(BF16))
            put_halves(s, levels + 1, total)
        total = mm(jnp.concatenate(image_b, axis=1), factors())
        leaf_norm = jnp.sum(total[:, :rank] * total[:, :rank], axis=1, keepdims=True)
        for level in range(levels):
            part = total[:, level * rank : (level + 1) * rank].astype(BF16)
            for s in range(slots):
                put(s, level, part)
        whole = mm(jnp.concatenate(image_b, axis=1), full_ref[...])
        second = [whole[:, s * rows : (s + 1) * rows] for s in range(slots)]
        for s in range(slots):
            put_halves(s, levels + 1 + 2 * (rows // rank), second[s])

        def dots(left, right):
            total = left[0] * right[0]
            for s in range(1, slots):
                total = total + left[s] * right[s]
            return jnp.sum(total, axis=1, keepdims=True)

        scalars = [
            dots(field, field),
            dots(field, image),
            dots(image, image),
            dots(image, second) + leaf_norm,
        ]
        lane = lax.broadcasted_iota(jnp.int32, (nrhs, rank), 1)
        packed = jnp.zeros((nrhs, rank), F32)
        for k, value in enumerate(scalars):
            value = jnp.broadcast_to(value, (nrhs, rank))
            for piece in range(3):
                rounded = value.astype(BF16).astype(F32)
                packed = jnp.where(lane == 3 * k + piece, rounded, packed)
                value = value - rounded
        for s in range(slots):
            put(s, levels, packed.astype(BF16))


def finish_kernel(leaves, field_ref, factors_ref, result_ref, *refs):
    sums = [refs[-m % leaves] for m in range(leaves)]
    solution_ref, residual_ref = refs[leaves:]
    levels, rows, rank = factors_ref.shape
    nrhs = field_ref.shape[0]
    field = field_ref[...]

    def halves(at):
        pieces = []
        for k in range(rows // rank):
            start = (at + 2 * k) * nrhs
            piece = result_ref[start : start + 2 * nrhs].astype(F32)
            pieces.append(piece[:nrhs] + piece[nrhs:])
        return jnp.concatenate(pieces, axis=1)

    image = halves(levels + 1)
    second = halves(levels + 1 + 2 * (rows // rank)) + 0.5 * image
    lane = lax.broadcasted_iota(jnp.int32, (nrhs, rank), 1)
    packed = sums[0][levels * nrhs :].astype(F32)
    for m in range(1, leaves):
        packed = packed + sums[m][(levels - 1) * nrhs :].astype(F32)

    def scalar(k):
        inside = (lane >= 3 * k) & (lane < 3 * k + 3)
        return jnp.sum(jnp.where(inside, packed, 0.0), axis=1, keepdims=True)

    bb, bw, ww, wu = (scalar(k) for k in range(4))
    wu = wu + 0.5 * ww
    for level in range(levels):
        nodes = {}
        for m in range(leaves if level else 1):
            at = level if m == 0 else level - 1
            value = sums[m][at * nrhs : (at + 1) * nrhs].astype(F32)
            node = m >> level
            nodes[node] = nodes[node] + value if node in nodes else value
        second = second + mm_nt(nodes[0].astype(BF16), factors_ref[level])
        if level > 0:
            squared = sum(value * value for value in nodes.values())
            wu = wu + jnp.sum(squared, axis=1, keepdims=True)
    alpha0 = bb / bw
    norm1 = alpha0 * alpha0 * ww - bb
    ratio = norm1 / bb
    keep = 1.0 + ratio
    curv = keep * keep * bw - 2.0 * keep * alpha0 * ww + alpha0 * alpha0 * wu
    alpha1 = norm1 / curv
    solution_ref[...] = (alpha0 + alpha1 * keep) * field - (alpha1 * alpha0) * image
    residual_ref[...] = field - (alpha0 + alpha1 * keep) * image + (alpha1 * alpha0) * second


def call(kernel, outs, args, specs, scratch=(), flops=0, limit=24, aliases={}):
    moved = sum(a.size * a.dtype.itemsize for a in args)
    return pl.pallas_call(
        kernel,
        out_shape=[jax.ShapeDtypeStruct(shape, dtype) for shape, dtype in outs],
        in_specs=specs,
        out_specs=[VMEM] * len(outs),
        scratch_shapes=list(scratch),
        input_output_aliases=aliases,
        cost_estimate=pl.CostEstimate(flops=flops, bytes_accessed=moved, transcendentals=0),
        compiler_params=pltpu.CompilerParams(vmem_limit_bytes=limit * 2**20),
    )(*args)


def collected(embed, factors, targets):
    leaves, inner = lax.axis_size("leaf"), lax.axis_size("inner")
    levels, rows, rank = factors.shape
    dims, nrhs = embed.shape[1], targets.shape[1]
    shape = (rows, dims, levels, rank, nrhs)

    def host(leaf):
        return inner // 2 if leaf % 2 == 0 else (inner - 1) // 2

    def others(leaf):
        sign = 1 if leaf % 2 == 0 else -1
        here = host(leaf)
        places = [z for z in range(inner) if z != here]
        places.sort(key=lambda z: (-abs(z - here), sign * z))
        if leaf % 2:
            places = places[-1:] + places[:-1]
        return places

    routes = [
        [(leaf * inner + others(leaf)[k], leaf * inner + host(leaf)) for leaf in range(leaves)]
        for k in range(inner - 1)
    ]

    axes = ("leaf", "inner")

    def to_host(value):
        return [value] + [lax.ppermute(value, axes, route) for route in routes]

    def over_leaf(value, m):
        return lax.ppermute(value, "leaf", [(i, i ^ m) for i in range(leaves)])

    field = targets.T
    near = inner - 1
    held, pairs = len(pairs_of(near)), len(pairs_of(inner))
    head = dims // rank * rows + 2 * nrhs * (rows // rank)
    tail = levels * (rows + 2 * nrhs)
    sizes = [((head, rank), BF16), ((tail, rank), BF16)]
    sizes += [((nrhs, rank), F32), (((levels - 1) * nrhs, rank), F32)]
    first_part, second_part, first, upper = call(
        pack_kernel, sizes, [embed, factors, field], [VMEM] * 3
    )
    heads = to_host(first_part)
    proj = [first]
    for bit in range(levels - 1):
        upper = upper + over_leaf(upper, 2**bit)
        proj.append(upper[:nrhs])
        upper = upper[nrhs:]
    (second_part,) = call(
        functools.partial(tail_kernel, levels * rows),
        [sizes[1]],
        [second_part] + proj,
        [VMEM] * (1 + levels),
        aliases={0: 0},
    )
    tails = to_host(second_part)
    leaf = lax.axis_index("leaf")
    here = jnp.where(leaf % 2 == 0, host(0), host(1))
    is_host = (lax.axis_index("inner") == here).astype(jnp.int32).reshape(1)
    near_high, near_image = call(
        functools.partial(near_kernel, near, shape),
        [((held, rows, rows), BF16), ((near, nrhs, rows), F32)],
        [is_host] + heads[:near],
        [SMEM] + [VMEM] * near,
        scratch=[pltpu.VMEM((held, rows, rows), BF16)],
        flops=NEAR_FLOPS,
    )
    full, image = call(
        functools.partial(far_kernel, inner, shape),
        [((inner * rows, inner * rows), BF16), ((inner, nrhs, rows), F32)],
        [is_host, near_high, near_image] + heads,
        [SMEM] + [VMEM] * (2 + inner),
        scratch=[pltpu.VMEM((pairs - held, rows, rows), BF16)] * 2,
        flops=FAR_FLOPS,
    )
    height = (levels + 1 + 4 * (rows // rank)) * nrhs
    results = call(
        functools.partial(main_kernel, inner, shape),
        [((height, rank), BF16)] * inner,
        [is_host, full, image] + heads + tails,
        [SMEM] + [VMEM] * (2 + 2 * inner),
        flops=MAIN_FLOPS,
    )
    result = results[0]
    for slot in [*range(2, inner), 1][: inner - 1]:
        route = [(b, a) for a, b in routes[slot - 1]]
        result = result + lax.ppermute(results[slot], axes, route)
    sums = result[: (levels + 1) * nrhs]
    above = sums[nrhs:]
    leaf_sums = [sums] + [over_leaf(above, m) for m in range(leaves - 1, 0, -1)]
    answer, residual = call(
        functools.partial(finish_kernel, leaves),
        [((nrhs, rows), F32)] * 2,
        [field, factors, result] + leaf_sums,
        [VMEM] * (3 + leaves),
    )
    return (answer.T, residual.T)


def on_device(embed, factors, targets):
    _, rows, rank = factors.shape
    whole = rows % rank == 0 and embed.shape[1] % rank == 0
    if whole and rows * lax.axis_size("inner") <= FAST_LEAF:
        return collected(embed, factors, targets)
    return stepwise(embed, factors, targets)


def solution(mesh):
    return jax.shard_map(
        on_device,
        mesh=mesh,
        in_specs=(
            P(("groups", "leaf", "inner"), None),
            P(None, ("groups", "leaf", "inner"), None),
            P(("groups", "leaf", "inner"), None),
        ),
        out_specs=(P(("groups", "leaf", "inner"), None), P(("groups", "leaf", "inner"), None)),
        check_vma=False,
    )
```
